32 devices in a mesh: page: 8 (over y, x, core), tok: 4 (over z).
Axes of the slice: x: 2, y: 2, z: 4, core: 2. Of those that a mesh axis runs over, the one named last changes fastest.
Arguments:
- tokens: bfloat16 [4480, 768], P(('page', 'tok')), may hold values from -6 to 6
- w_query: bfloat16 [768, 768], replicated, may hold values from -0.21875 to 0.21875
- w_key: bfloat16 [768, 768], replicated, may hold values from -0.21875 to 0.21875
- w_value: bfloat16 [768, 768], replicated, may hold values from -0.21875 to 0.21875
- w_out: bfloat16 [768, 768], replicated, may hold values from -1.75 to 1.75
- w_inner: bfloat16 [768, 3072], replicated, may hold values from -0.21875 to 0.21875
- w_outer: bfloat16 [3072, 768], replicated, may hold values from -0.109375 to 0.109375
- gain_one: float32 [768], replicated, may hold values from 0.5 to 1.5
- shift_one: float32 [768], replicated, may hold values from -3 to 3
- gain_two: float32 [768], replicated, may hold values from 0.5 to 1.5
- shift_two: float32 [768], replicated, may hold values from -3 to 3
- table_line: float32 [12, 32], replicated, may hold values from -3 to 3
- table_horiz: float32 [12, 32], replicated, may hold values from -3 to 3
- table_vert: float32 [12, 32], replicated, may hold values from -3 to 3
- region_weight: float32 [12], replicated, may hold values from -3 to 3
- region_ids: int32 [4480], P(('page', 'tok')), may hold values from 0 to 59
- line_pos: int32 [4480], P(('page', 'tok')), may hold values from 0 to 559
- box_horiz: int32 [4480], P(('page', 'tok')), may hold values from 0 to 63
- box_vert: int32 [4480], P(('page', 'tok')), may hold values from 0 to 63
- cotangent: bfloat16 [4480, 768], P(('page', 'tok')), may hold values from -6 to 6
Outputs:
- block_out: bfloat16 [4480, 768], P(('page', 'tok'))
- d_tokens: bfloat16 [4480, 768], P(('page', 'tok'))
- grad_w_query: float32 [768, 768], P(('page', 'tok'))
- grad_w_key: float32 [768, 768], P(('page', 'tok'))
- grad_w_value: float32 [768, 768], P(('page', 'tok'))
- grad_w_out: float32 [768, 768], P(('page', 'tok'))
- grad_w_inner: float32 [768, 3072], P(('page', 'tok'))
- grad_w_outer: float32 [3072, 768], P(('page', 'tok'))
- grad_gain_one: float32 [768], replicated
- grad_shift_one: float32 [768], replicated
- grad_gain_two: float32 [768], replicated
- grad_shift_two: float32 [768], replicated
- grad_table_line: float32 [12, 32], replicated
- grad_table_horiz: float32 [12, 32], replicated
- grad_table_vert: float32 [12, 32], replicated
- grad_region_weight: float32 [12], replicated
The draws below stay inside these ranges and needn't reach their ends.
All inputs are finite; a program needn't handle non-finite values.
Results may differ from the reference program's by a relative error of at most 0.02.
Values may be sent and summed in bfloat16 or wider, within the bound.
No kernel may reach another device: no remote copies, remote signals or barrier semaphores. Data moves between devices by JAX's collectives and lax.ppermute only.
A program may use at most 128 MiB of HBM per device.

```python
import math
import jax
import jax.numpy as jnp
import numpy as np
from jax import lax

D = 768
HEADS = 12
FF = 3072
TEXT = 512
PATCH = 48
REL = 32
BOXES = 64
REGIONS = 60
PAGES_GRP = 1
TOKENS = 4480
N_PAGE = 8


def with_ends(drawn, stream_key, smallest, high):
    extent = drawn.shape
    spot = [jax.random.randint(jax.random.fold_in(stream_key, axis), (), 0, extent[axis]) for axis in range(len(extent))]
    drawn = drawn.at[tuple(spot)].set(smallest)
    longest = extent.index(max(extent))
    spot[longest] = (spot[longest] + 1) % extent[longest]
    return drawn.at[tuple(spot)].set(high)


def with_spikes(values, rng, source, target, blocks, factor):
    owner, partner = [(jnp.arange(values.shape[dim]) // (values.shape[dim] // blocks)).reshape([-1 if axis == dim else 1 for axis in range(values.ndim)]) for dim in (source, target)]
    chosen = jax.random.permutation(rng, blocks)[partner]
    strong = (owner == chosen) | (owner == (partner + blocks // 2) % blocks)
    return jnp.where(strong, factor * values, values)


def levels(key, dims, split, smallest, top_value):
    def one(axis_at, blocks):
        steps = jax.random.uniform(jax.random.fold_in(jax.random.fold_in(key, 6), axis_at), (blocks,), jnp.float32, smallest / len(split), top_value / len(split))
        return jnp.repeat(jnp.exp(steps), dims[axis_at] // blocks).reshape((-1,) + (1,) * (len(dims) - axis_at - 1))

    loudness = one(*split[0])
    for cut in split[1:]:
        loudness = loudness * one(*cut)
    return loudness


def cumulative_ranks(count, lean):
    loads = [(1 << 20) // math.isqrt(grade ** lean) + 1 for grade in range(1, count + 1)]
    scale = 1 + sum(loads) // (1 << 30)
    return np.cumsum(np.array([max(1, weight // scale) for weight in loads]))


def ranked(stream_key, extent, number_of, skew):
    grid = cumulative_ranks(number_of, skew)
    pick = jax.random.randint(jax.random.fold_in(stream_key, 1), extent, 0, int(grid[number_of - 1]))
    rank = jnp.searchsorted(jnp.asarray(grid, jnp.int32), pick, side="right")
    return jax.random.permutation(jax.random.fold_in(stream_key, 2), number_of)[rank].astype(jnp.int32)


def centred(stream_key, extent, width, most, split=(), kind=jnp.bfloat16):
    factor_of = levels(stream_key, extent, split, -0.22, 0.18) if split else 1.0
    values = jax.random.normal(stream_key, extent, jnp.float32) * width * factor_of
    return jnp.minimum(jnp.maximum(values, -most), most).astype(kind)


def bell_draw_with(key, shape, scale, bound, cuts, heavy, kind=jnp.bfloat16):
    values = scale * jax.random.normal(key, shape, jnp.float32)
    if cuts:
        values = values * levels(key, shape, cuts, -0.22, 0.18)
    return jnp.clip(with_spikes(values, jax.random.fold_in(key, 3), *heavy), -bound, bound).astype(kind)


def setup_inputs(seed: int = 0) -> dict:
    keys = jax.random.split(jax.random.key(seed), 21)
    tokens = bell_draw_with(keys[0], (TOKENS, D), 1.0, 6.0, ((0, 32),), (0, 1, 32, 2.75))
    w_query = centred(keys[1], (D, D), D ** -0.5, 0.21875)
    w_key = centred(keys[2], (D, D), D ** -0.5, 0.21875)
    w_value = centred(keys[3], (D, D), D ** -0.5, 0.21875)
    w_out = centred(keys[4], (D, D), (D // 64) ** -0.5, 1.75)
    w_inner = centred(keys[5], (D, FF), D ** -0.5, 0.21875)
    w_outer = centred(keys[6], (FF, D), FF ** -0.5, 0.109375)
    gain_one = jnp.clip(1.0 + 0.1 * jax.random.normal(keys[7], (D,), jnp.float32), 0.5, 1.5)
    shift_one = centred(keys[8], (D,), 0.3, 3.0, (), jnp.float32)
    gain_two = jnp.clip(1.0 + 0.1 * jax.random.normal(keys[9], (D,), jnp.float32), 0.5, 1.5)
    shift_two = centred(keys[10], (D,), 0.3, 3.0, (), jnp.float32)
    table_line = centred(keys[11], (HEADS, REL), 0.5, 3.0, (), jnp.float32)
    table_horiz = centred(keys[12], (HEADS, REL), 0.5, 3.0, (), jnp.float32)
    table_vert = centred(keys[13], (HEADS, REL), 0.5, 3.0, (), jnp.float32)
    region_weight = centred(keys[14], (HEADS,), 0.7, 3.0, (), jnp.float32)
    region_ids = with_ends(ranked(keys[15], (TOKENS,), REGIONS, 2), jax.random.fold_in(keys[15], 3), 0, REGIONS - 1).astype(jnp.int32)
    line_pos = with_ends(jax.random.randint(keys[16], (TOKENS,), 0, TEXT + PATCH), jax.random.fold_in(keys[16], 1), 0, (TEXT + PATCH) - 1).astype(jnp.int32)
    box_horiz = with_ends(jax.random.randint(keys[17], (TOKENS,), 0, BOXES), jax.random.fold_in(keys[17], 1), 0, BOXES - 1).astype(jnp.int32)
    box_vert = with_ends(jax.random.randint(keys[18], (TOKENS,), 0, BOXES), jax.random.fold_in(keys[18], 1), 0, BOXES - 1).astype(jnp.int32)
    cotangent = centred(keys[19], (TOKENS, D), 1.0, 6.0, ((0, 32),))
    return dict(tokens=tokens, w_query=w_query, w_key=w_key, w_value=w_value, w_out=w_out, w_inner=w_inner, w_outer=w_outer, gain_one=gain_one, shift_one=shift_one, gain_two=gain_two, shift_two=shift_two, table_line=table_line, table_horiz=table_horiz, table_vert=table_vert, region_weight=region_weight, region_ids=region_ids, line_pos=line_pos, box_horiz=box_horiz, box_vert=box_vert, cotangent=cotangent)


@jax.custom_vjp
def low(v):
    return lax.optimization_barrier(v.astype(jnp.bfloat16)).astype(jnp.float32)

@jax.custom_vjp
def low_back(v):
    return v

def low_keep(v):
    return (low(v), None)

def low_pass(kept, grad):
    return (grad,)

def back_keep(v):
    return (v, None)

def back_low(kept, grad):
    return (low(grad),)
low.defvjp(low_keep, low_pass)
low_back.defvjp(back_keep, back_low)
HIGH = lax.Precision.HIGHEST

def both_round(value_in):
    return low_back(low(value_in))

def norm_rows(value_in, gain_vec, shift_vec):
    row_mean = lax.optimization_barrier(jnp.mean(value_in, axis=-1, keepdims=True))
    centered = value_in - row_mean
    variance = lax.optimization_barrier(jnp.mean(centered * centered, axis=-1, keepdims=True))
    return centered * lax.rsqrt(variance + 1e-05) * gain_vec + shift_vec

def bucket_of(query_at, key_at):
    half_span = REL // 2
    return jnp.clip(key_at[None, :] - query_at[:, None], -half_span, half_span - 1) + half_span

def rel_bias(tables, query_places, key_places):
    table_line, table_horiz, table_vert, region_weight = tables
    bias_sum = jnp.take(table_line, bucket_of(query_places[1], key_places[1]), axis=1)
    bias_sum = bias_sum + jnp.take(table_horiz, bucket_of(query_places[2], key_places[2]), axis=1)
    bias_sum = bias_sum + jnp.take(table_vert, bucket_of(query_places[3], key_places[3]), axis=1)
    same_region = (query_places[0][:, None] == key_places[0][None, :]).astype(table_line.dtype)
    return bias_sum + region_weight[:, None, None] * same_region[None]

def page_order():
    text_total = PAGES_GRP * TEXT
    pieces = []
    for page_index in range(PAGES_GRP):
        pieces.append(np.arange(page_index * TEXT, (page_index + 1) * TEXT))
        pieces.append(text_total + np.arange(page_index * PATCH, (page_index + 1) * PATCH))
    return np.concatenate(pieces).astype(np.int32)

def group_forward(x_pages, params, places):
    w_query, w_key, w_value, w_out, w_inner, w_outer, gain_one, shift_one, gain_two, shift_two, table_line, table_horiz, table_vert, region_weight = params
    page_count, length, model_width = x_pages.shape
    head_count = table_line.shape[0]
    head_dim = model_width // head_count
    queries = both_round(jnp.einsum('pld,de->ple', x_pages, w_query, precision=HIGH))
    queries = queries.reshape(page_count, length, head_count, head_dim)
    keys_page = both_round(jnp.einsum('pld,de->ple', x_pages, w_key, precision=HIGH))
    keys_page = keys_page.reshape(page_count, length, head_count, head_dim)
    values_page = both_round(jnp.einsum('pld,de->ple', x_pages, w_value, precision=HIGH))
    values_page = values_page.reshape(page_count, length, head_count, head_dim)
    tables = (table_line, table_horiz, table_vert, region_weight)
    bias_sum = jax.vmap(lambda one_places: rel_bias(tables, one_places, one_places))(places)
    scores = jnp.einsum('pqhd,pkhd->phqk', queries, keys_page, precision=HIGH) * 0.125 + bias_sum
    scores = low_back(scores)
    row_max = lax.optimization_barrier(jnp.max(scores, axis=-1, keepdims=True))
    exponent = jnp.exp(scores - row_max)
    weights_soft = low(exponent / lax.optimization_barrier(jnp.sum(exponent, axis=-1, keepdims=True)))
    heads_mix = jnp.einsum('phqk,pkhd->pqhd', weights_soft, values_page, precision=HIGH)
    heads_mix = both_round(heads_mix.reshape(page_count, length, model_width))
    attn_out = low_back(jnp.einsum('pld,de->ple', heads_mix, w_out, precision=HIGH))
    hidden = norm_rows(x_pages + attn_out, gain_one, shift_one)
    inner = low_back(jnp.einsum('pld,df->plf', low(hidden), w_inner, precision=HIGH))
    active = low(jax.nn.gelu(inner, approximate=False))
    outer_out = low_back(jnp.einsum('plf,fd->pld', active, w_outer, precision=HIGH))
    return norm_rows(hidden + outer_out, gain_two, shift_two)

def reference(tokens, w_query, w_key, w_value, w_out, w_inner, w_outer, gain_one, shift_one, gain_two, shift_two, table_line, table_horiz, table_vert, region_weight, region_ids, line_pos, box_horiz, box_vert, cotangent):
    row_order = page_order()
    row_back = np.argsort(row_order).astype(np.int32)
    group_rows = row_order.shape[0]
    length = TEXT + PATCH

    def to_pages(array_in):
        grouped = array_in.reshape((N_PAGE, group_rows) + array_in.shape[1:])[:, row_order]
        return grouped.reshape((N_PAGE, PAGES_GRP, length) + array_in.shape[1:])

    def from_pages(array_in):
        grouped = array_in.reshape((N_PAGE, group_rows) + array_in.shape[3:])[:, row_back]
        return grouped.reshape((N_PAGE * group_rows,) + array_in.shape[3:])
    places = jnp.stack([region_ids, line_pos, box_horiz, box_vert], -1).astype(jnp.int32)
    places = jnp.moveaxis(to_pages(places), -1, 2)
    x_all = to_pages(tokens.astype(jnp.float32))
    cot_all = to_pages(cotangent.astype(jnp.float32))
    params = (w_query.astype(jnp.float32), w_key.astype(jnp.float32), w_value.astype(jnp.float32), w_out.astype(jnp.float32), w_inner.astype(jnp.float32), w_outer.astype(jnp.float32), gain_one, shift_one, gain_two, shift_two, table_line, table_horiz, table_vert, region_weight)

    def group_step(grad_sum, group_items):
        x_group, places_group, cot_group = group_items
        group_out, pullback = jax.vjp(lambda x_in, param_in: group_forward(x_in, param_in, places_group), x_group, params)
        d_input, d_params = pullback(cot_group)
        grad_sum = jax.tree.map(lambda left, right: left + right, grad_sum, d_params)
        return (grad_sum, (group_out, d_input))
    zero_grads = jax.tree.map(jnp.zeros_like, params)
    total_grads, (all_out, all_dinput) = lax.scan(group_step, zero_grads, (x_all, places, cot_all))
    return (from_pages(all_out).astype(jnp.bfloat16), from_pages(all_dinput).astype(jnp.bfloat16), total_grads[0], total_grads[1], total_grads[2], total_grads[3], total_grads[4], total_grads[5], total_grads[6], total_grads[7], total_grads[8], total_grads[9], total_grads[10], total_grads[11], total_grads[12], total_grads[13])
```

```python
import jax
import jax.numpy as jnp
from jax import lax
from jax.sharding import PartitionSpec as P

TEXT = 512
PATCH = 48
REL = 32
PAGES_GRP = 1


HIGH = lax.Precision.HIGHEST


def norm_rows(value_in, gain_vec, shift_vec):
    row_mean = jnp.mean(value_in, axis=-1, keepdims=True)
    centered = value_in - row_mean
    variance = jnp.mean(centered * centered, axis=-1, keepdims=True)
    return centered * lax.rsqrt(variance + 1e-05) * gain_vec + shift_vec


def exact_gelu(value_in):
    return jax.nn.gelu(value_in, approximate=False)


def bucket_of(query_at, key_at):
    half_span = REL // 2
    return jnp.clip(key_at[None, :] - query_at[:, None], -half_span, half_span - 1) + half_span


def place_hots(query_places, key_places):
    levels = jnp.arange(REL, dtype=jnp.int32)
    hots = []
    for which in range(1, 4):
        bucket = bucket_of(query_places[which], key_places[which])
        hots.append((bucket[:, :, None] == levels[None, None, :]).astype(jnp.bfloat16))
    same_region = (query_places[0][:, None] == key_places[0][None, :]).astype(jnp.float32)
    return (hots, same_region)


def bias_from(tables, hots, same_region):
    table_line, table_horiz, table_vert, region_weight = tables
    bias_sum = region_weight[:, None, None] * same_region[None]
    for table_one, hot_one in (
        (table_line, hots[0]),
        (table_horiz, hots[1]),
        (table_vert, hots[2]),
    ):
        bias_sum = bias_sum + jnp.einsum(
            "hb,qkb->hqk", table_one, hot_one.astype(jnp.float32), precision=HIGH
        )
    return bias_sum


def bias_grads(d_scores, hots, same_region):
    grads = [
        jnp.einsum("hqk,qkb->hb", d_scores, hot_one, preferred_element_type=jnp.float32)
        for hot_one in hots
    ]
    region_grad = jnp.sum(d_scores.astype(jnp.float32) * same_region[None], axis=(1, 2))
    return (grads[0], grads[1], grads[2], region_grad)


def swap(array_in, axis_name, flip):
    size = lax.axis_size(axis_name)
    return lax.ppermute(array_in, axis_name, [(at, at ^ flip) for at in range(size)])


def tok_shards(array_in):
    return [array_in] + [swap(array_in, "tok", step) for step in range(1, lax.axis_size("tok"))]


def page_bits():
    size = lax.axis_size("page")
    bits = [1 << at for at in range(size.bit_length() - 1)]
    return bits


def reduce_page(blocks, bits):
    left = sorted(bits, reverse=True)
    for bit in bits:
        axis = left.index(bit)
        keep = lax.index_in_dim(blocks, 0, axis, keepdims=False)
        send = lax.index_in_dim(blocks, 1, axis, keepdims=False)
        blocks = keep + swap(send, "page", bit)
        left.remove(bit)
    return blocks


def reduce_grad(terms):
    page_count, rows, cols = terms.shape
    bits = page_bits()
    cube = terms.reshape((2,) * len(bits) + (rows, cols))
    half = cols // 2
    one = reduce_page(cube[..., :half], bits)
    two = reduce_page(cube[..., half:], bits[:1] + bits[:0:-1])
    tok_count = lax.axis_size("tok")
    tok_index = lax.axis_index("tok")
    share = rows // tok_count
    outs = []
    for part in (one, two):
        total = None
        for step in range(tok_count):
            piece = lax.dynamic_slice_in_dim(part, (tok_index ^ step) * share, share, 0)
            if step:
                piece = swap(piece, "tok", step)
            piece = piece.astype(jnp.float32)
            total = piece if total is None else total + piece
        outs.append(total)
    return jnp.concatenate(outs, 1)


def xor_blocks(array_t):
    page_count = lax.axis_size("page")
    page_index = lax.axis_index("page")
    share = array_t.shape[0] // page_count
    return jnp.stack(
        [
            lax.dynamic_slice_in_dim(array_t, (page_index ^ step) * share, share, 0)
            for step in range(page_count)
        ]
    )


def grad_terms(left, right):
    blocks = xor_blocks(left.T)
    return jnp.einsum("prk,kc->prc", blocks, right, preferred_element_type=jnp.float32).astype(
        jnp.bfloat16
    )


def sum_all(vector):
    for bit in page_bits():
        vector = vector + swap(vector, "page", bit)
    step = 1
    while step < lax.axis_size("tok"):
        vector = vector + swap(vector, "tok", step)
        step *= 2
    return vector


def on_device(
    tokens,
    w_query,
    w_key,
    w_value,
    w_out,
    w_inner,
    w_outer,
    gain_one,
    shift_one,
    gain_two,
    shift_two,
    table_line,
    table_horiz,
    table_vert,
    region_weight,
    region_ids,
    line_pos,
    box_horiz,
    box_vert,
    cotangent,
):
    row_count, model_width = tokens.shape
    head_count = table_line.shape[0]
    head_dim = model_width // head_count
    tables = (table_line, table_horiz, table_vert, region_weight)
    own_places = jnp.stack([region_ids, line_pos, box_horiz, box_vert], 0)
    all_places = jnp.concatenate(tok_shards(own_places), 1)
    tokens_all = jnp.concatenate(tok_shards(tokens), 0)
    all_rows = tokens_all.shape[0]

    def project(rows, weight):
        return jnp.dot(rows, weight, preferred_element_type=jnp.float32).astype(jnp.bfloat16)

    def heads(array_in):
        return array_in.reshape(array_in.shape[0], head_count, head_dim)

    query = heads(project(tokens, w_query))
    keys_all = heads(project(tokens_all, w_key))
    values_all = heads(project(tokens_all, w_value))
    hots, same_region = place_hots(own_places, all_places)
    scores = (
        jnp.einsum("qhd,khd->hqk", query, keys_all, preferred_element_type=jnp.float32) * 0.125
        + bias_from(tables, hots, same_region)
    )
    row_max = jnp.max(scores, axis=-1, keepdims=True)
    exponent = jnp.exp(scores - row_max)
    probs = exponent / jnp.sum(exponent, axis=-1, keepdims=True)
    weights_low = probs.astype(jnp.bfloat16)
    heads_mix = jnp.einsum(
        "hqk,khd->qhd", weights_low, values_all, preferred_element_type=jnp.float32
    )
    heads_low = heads_mix.reshape(row_count, model_width).astype(jnp.bfloat16)
    attn_out = jnp.dot(heads_low, w_out, preferred_element_type=jnp.float32)
    hidden, norm_one_pull = jax.vjp(
        norm_rows, tokens.astype(jnp.float32) + attn_out, gain_one, shift_one
    )
    hidden_low = hidden.astype(jnp.bfloat16)
    inner = jnp.dot(hidden_low, w_inner, preferred_element_type=jnp.float32)
    active, gelu_pull = jax.vjp(exact_gelu, inner)
    active_low = active.astype(jnp.bfloat16)
    outer_out = jnp.dot(active_low, w_outer, preferred_element_type=jnp.float32)
    result, norm_two_pull = jax.vjp(norm_rows, hidden + outer_out, gain_two, shift_two)
    block_out = result.astype(jnp.bfloat16)
    d_second, d_gain_two, d_shift_two = norm_two_pull(cotangent.astype(jnp.float32))
    d_outer = d_second.astype(jnp.bfloat16)
    grad_w_outer = reduce_grad(grad_terms(active_low, d_outer))
    d_active = jnp.einsum("rd,fd->rf", d_outer, w_outer, preferred_element_type=jnp.float32)
    d_inner = gelu_pull(d_active)[0].astype(jnp.bfloat16)
    grad_w_inner = reduce_grad(grad_terms(hidden_low, d_inner))
    d_hidden = d_second + jnp.einsum(
        "rf,df->rd", d_inner, w_inner, preferred_element_type=jnp.float32
    )
    d_first, d_gain_one, d_shift_one = norm_one_pull(d_hidden)
    d_attn = d_first.astype(jnp.bfloat16)
    grad_w_out = reduce_grad(grad_terms(heads_low, d_attn))
    d_heads = jnp.einsum("re,de->rd", d_attn, w_out, preferred_element_type=jnp.float32)
    d_heads = heads(d_heads.astype(jnp.bfloat16))

    d_weights = jnp.einsum("qhd,khd->hqk", d_heads, values_all, preferred_element_type=jnp.float32)
    row_dot = jnp.sum(probs * d_weights, axis=-1, keepdims=True)
    d_scores = (probs * (d_weights - row_dot)).astype(jnp.bfloat16)
    d_query = 0.125 * jnp.einsum(
        "hqk,khd->qhd", d_scores, keys_all, preferred_element_type=jnp.float32
    )
    d_key = 0.125 * jnp.einsum("hqk,qhd->khd", d_scores, query, preferred_element_type=jnp.float32)
    d_value = jnp.einsum("hqk,qhd->khd", weights_low, d_heads, preferred_element_type=jnp.float32)
    d_tables = bias_grads(d_scores, hots, same_region)
    d_query = d_query.reshape(row_count, model_width).astype(jnp.bfloat16)
    d_key = d_key.reshape(all_rows, model_width).astype(jnp.bfloat16)
    d_value = d_value.reshape(all_rows, model_width).astype(jnp.bfloat16)

    def back(rows, weight):
        return jnp.einsum("re,de->rd", rows, weight, preferred_element_type=jnp.float32)

    d_rows = (back(d_key, w_key) + back(d_value, w_value)).astype(jnp.bfloat16)
    d_input = d_first + back(d_query, w_query)
    for step in range(lax.axis_size("tok")):
        piece = d_rows[step * row_count : (step + 1) * row_count]
        if step:
            piece = swap(piece, "tok", step)
        d_input = d_input + piece.astype(jnp.float32)
    d_tokens = d_input.astype(jnp.bfloat16)
    grad_w_query = reduce_grad(grad_terms(tokens, d_query))
    grad_w_key = reduce_grad(grad_terms(tokens_all, d_key))
    grad_w_value = reduce_grad(grad_terms(tokens_all, d_value))

    small = (d_gain_one, d_shift_one, d_gain_two, d_shift_two) + tuple(d_tables)
    flat = jnp.concatenate([item.reshape(-1) for item in small])
    lanes = 128
    padded = -(-flat.shape[0] // (8 * lanes)) * 8 * lanes
    flat = jnp.pad(flat, (0, padded - flat.shape[0])).reshape(-1, lanes)
    flat = sum_all(flat).reshape(-1)
    summed, place = [], 0
    for item in small:
        summed.append(flat[place : place + item.size].reshape(item.shape))
        place += item.size
    return (
        block_out,
        d_tokens,
        grad_w_query,
        grad_w_key,
        grad_w_value,
        grad_w_out,
        grad_w_inner,
        grad_w_outer,
        *summed,
    )


def solution(mesh):
    placed = (
        P(("page", "tok"), None),
        P(),
        P(),
        P(),
        P(),
        P(),
        P(),
        P(),
        P(),
        P(),
        P(),
        P(),
        P(),
        P(),
        P(),
        P(("page", "tok")),
        P(("page", "tok")),
        P(("page", "tok")),
        P(("page", "tok")),
        P(("page", "tok"), None),
    )
    return jax.shard_map(
        on_device,
        mesh=mesh,
        in_specs=placed,
        out_specs=(
            P(("page", "tok"), None),
            P(("page", "tok"), None),
            P(("page", "tok"), None),
            P(("page", "tok"), None),
            P(("page", "tok"), None),
            P(("page", "tok"), None),
            P(("page", "tok"), None),
            P(("page", "tok"), None),
            P(),
            P(),
            P(),
            P(),
            P(),
            P(),
            P(),
            P(),
        ),
        check_vma=False,
    )
```

```python
import math

import jax
import jax.numpy as jnp
from jax import lax
from jax.experimental import pallas as pl
from jax.experimental.pallas import tpu as pltpu
from jax.sharding import PartitionSpec as P

REL = 32
BOXES = 64
BF = jnp.bfloat16
F32 = jnp.float32
I32 = jnp.int32
NEG = -1e30
LANES = 128
MIB = 2**20


def vmem():
    return pl.BlockSpec(memory_space=pltpu.VMEM)


def smem():
    return pl.BlockSpec(memory_space=pltpu.SMEM)


def like(shape, kind):
    return jax.ShapeDtypeStruct(shape, kind)


def launch(kernel, operands, in_specs, name, limit, out_shape, scratch_shapes=(), after=()):
    count = len(operands)

    def body(*refs):
        kernel(*refs[:count], *refs[count + len(after) :])

    return pl.pallas_call(
        body,
        out_shape=out_shape,
        in_specs=in_specs + [pl.BlockSpec(memory_space=pl.ANY)] * len(after),
        out_specs=[vmem()] * len(out_shape),
        scratch_shapes=list(scratch_shapes),
        compiler_params=pltpu.CompilerParams(vmem_limit_bytes=limit * MIB),
        name=name,
    )(*operands, *after)


def dot_nn(left, right):
    return lax.dot_general(left, right, (((1,), (0,)), ((), ())), preferred_element_type=F32)


def dot_nt(left, right):
    return lax.dot_general(left, right, (((1,), (1,)), ((), ())), preferred_element_type=F32)


def look(table_row, index):
    return jnp.take_along_axis(jnp.broadcast_to(table_row, index.shape), index, axis=1)


def two_parts(value):
    high = value.astype(BF)
    return high, (value - high.astype(F32)).astype(BF)


def key_places(info, shard, rows, keys):
    pieces = []
    for at in range(3):
        wide = jnp.concatenate(
            [info[:, at * 256 : (at + 1) * 256], jnp.zeros((16, keys - 256), F32)], 1
        )
        pieces.append(pltpu.roll(wide, shard * rows, 1) if shard else wide)
    return pieces


def line_index(query_at, key_at):
    bucket = jnp.clip(key_at[1:2, :] - query_at[:, 1:2], -(REL // 2), REL // 2 - 1) + REL // 2
    same = jnp.where(query_at[:, 0:1] == key_at[0:1, :], REL, 0)
    return jnp.where(key_at[4:5, :] > 0, bucket + same, 2 * REL)


def attn_forward(
    token_shards, row_count, w_query, w_key, w_value, line_table, box_table, query_at
):
    rows, width = token_shards[0].shape
    head_count = line_table.shape[0]
    shards = len(token_shards)
    keys = -(-rows * shards // LANES) * LANES

    def kernel(*refs):
        tok_refs = refs[:shards]
        wq, wk, wv, line_ref, box_ref, q_at = refs[shards : shards + 6]
        mix_ref, q_ref, k_ref, v_ref, x_ref, p_ref, k_at, line_idx, box_idx, hots = refs[
            shards + 6 :
        ]
        places = [jnp.zeros((16, keys), F32)] * 3
        for at in range(shards):
            info = tok_refs[at][rows - 16 :, :].astype(F32)
            places = [
                left + right for left, right in zip(places, key_places(info, at, rows, keys))
            ]
        lane = lax.broadcasted_iota(I32, (1, keys), 1)
        live = jnp.zeros((1, keys), I32)
        for at in range(shards):
            inside = (lane >= at * rows) & (lane < at * rows + row_count)
            live = jnp.where(inside, 1, live)
        k_at[...] = jnp.zeros_like(k_at)
        k_at[0:1] = places[0][14:15].astype(I32)
        k_at[1:2] = (places[1][14:15] * 32.0 + places[2][14:15]).astype(I32)
        k_at[2:3] = places[0][15:16].astype(I32)
        k_at[3:4] = places[1][15:16].astype(I32)
        k_at[4:5] = live
        for at in range(shards):
            x_ref[at * rows : (at + 1) * rows] = tok_refs[at][...]
        if keys > shards * rows:
            x_ref[shards * rows :] = jnp.zeros((keys - shards * rows, width), BF)
        q_ref[...] = (dot_nn(tok_refs[0][...], wq[...]) * 0.125).astype(BF)
        k_ref[...] = dot_nn(x_ref[...], wk[...]).astype(BF)
        v_ref[...] = dot_nn(x_ref[...], wv[...]).astype(BF)
        line_idx[...] = line_index(q_at, k_at)
        lane = lax.broadcasted_iota(I32, (rows, LANES), 1)
        place = jnp.where(lane < BOXES, q_at[:, 2:3], q_at[:, 3:4])
        bucket = jnp.clip((lane & (BOXES - 1)) - place, -(REL // 2), REL // 2 - 1) + REL // 2
        box_idx[...] = bucket + jnp.where(lane < BOXES, 0, REL)
        sub = lax.broadcasted_iota(I32, (LANES, keys), 0)
        place = jnp.where(sub < BOXES, k_at[2:3, :], k_at[3:4, :])
        hot = ((sub & (BOXES - 1)) == place).astype(F32).astype(BF)
        hots[0:LANES] = hot
        hots[LANES:] = hot

        def pair(at, carry):
            col = pl.ds(pl.multiple_of(at * LANES, LANES), LANES)
            q_pair, k_pair, v_pair = q_ref[:, col], k_ref[:, col], v_ref[:, col]
            mixed = []
            for half in range(2):
                head = 2 * at + half
                mine = (lane < 64) if half == 0 else (lane >= 64)
                q_one = jnp.where(mine, q_pair, jnp.zeros_like(q_pair))
                high, low = two_parts(look(box_ref[pl.ds(head, 1), :], box_idx[...]))
                score = dot_nt(q_one, k_pair) + dot_nn(jnp.concatenate([high, low], 1), hots[...])
                line_row = line_ref[pl.ds(head, 1), :]
                score = score + jnp.concatenate(
                    [
                        look(line_row, line_idx[:, cut : cut + LANES])
                        for cut in range(0, keys, LANES)
                    ],
                    1,
                )
                grown = jnp.exp(score - jnp.max(score, axis=1, keepdims=True))
                probs = grown * (1.0 / jnp.sum(grown, axis=1, keepdims=True))
                low_probs = probs.astype(BF)
                p_ref[pl.ds(head, 1)] = low_probs[None]
                mixed.append(dot_nn(low_probs, v_pair))
            mix_ref[:, col] = jnp.where(lane < 64, mixed[0], mixed[1]).astype(BF)
            return carry

        lax.fori_loop(0, width // LANES, pair, 0)

    return launch(
        kernel,
        (*token_shards, w_query, w_key, w_value, line_table, box_table, query_at),
        [vmem()] * (shards + 6),
        "attn_forward",
        8,
        (
            like((rows, width), BF),
            like((rows, width), BF),
            like((keys, width), BF),
            like((keys, width), BF),
            like((keys, width), BF),
            like((head_count, rows, keys), BF),
            like((8, keys), I32),
        ),
        [
            pltpu.VMEM((rows, keys), I32),
            pltpu.VMEM((rows, LANES), I32),
            pltpu.VMEM((2 * LANES, keys), BF),
        ],
    )


def row_mean(value):
    return jnp.mean(value, axis=1, keepdims=True)


def all_sum(value):
    return jnp.sum(jnp.sum(value, axis=1, keepdims=True), axis=0, keepdims=True)


def normal(value):
    centered = value - row_mean(value)
    scale = lax.rsqrt(row_mean(centered * centered) + 1e-05)
    return centered * scale, scale


def normal_back(d_normal, n, scale):
    return scale * (d_normal - row_mean(d_normal) - n * row_mean(d_normal * n))


FF_CUT = 512


def feed_forward(mix, tokens, w_out, w_inner, w_outer, vectors, cotangent):
    rows, width = tokens.shape
    hidden_units = w_inner.shape[1]

    def kernel(mix_ref, tok, wo, wi, wu, vec, cot, *outs):
        block, hid, n_one, r_one, act, slope, d_sec, d_out, sums, total = outs
        n, r = normal(tok[...].astype(F32) + dot_nn(mix_ref[...], wo[...]))
        n_one[...] = n
        r_one[...] = jnp.broadcast_to(r, r_one.shape)
        hidden = n * vec[0:1, :] + vec[1:2, :]
        hid[...] = hidden.astype(BF)
        total[...] = hidden
        for cut in range(0, hidden_units, FF_CUT):
            inner = dot_nn(hid[...], wi[:, cut : cut + FF_CUT])
            upper = 0.5 + 0.5 * lax.erf(inner * (0.5**0.5))
            active = (inner * upper).astype(BF)
            act[:, cut : cut + FF_CUT] = active
            bell = jnp.exp(-0.5 * inner * inner) * (2.0 * math.pi) ** -0.5
            slope[:, cut : cut + FF_CUT] = upper + inner * bell
            total[...] += dot_nn(active, wu[cut : cut + FF_CUT, :])
        n, r = normal(total[...])
        block[...] = (n * vec[2:3, :] + vec[3:4, :]).astype(BF)
        grad = cot[...].astype(F32)
        sums[0:1, :] = jnp.sum(grad * n, axis=0, keepdims=True)
        sums[1:2, :] = jnp.sum(grad, axis=0, keepdims=True)
        second = normal_back(grad * vec[2:3, :], n, r)
        d_sec[...] = second
        d_out[...] = second.astype(BF)

    return launch(
        kernel,
        (mix, tokens, w_out, w_inner, w_outer, vectors, cotangent),
        [vmem()] * 7,
        "feed_forward",
        10,
        (
            like((rows, width), BF),
            like((rows, width), BF),
            like((rows, width), F32),
            like((rows, LANES), F32),
            like((rows, hidden_units), BF),
            like((rows, hidden_units), F32),
            like((rows, width), F32),
            like((rows, width), BF),
            like((2, width), F32),
        ),
        [pltpu.VMEM((rows, width), F32)],
    )


def feed_back(d_outer, d_second, slope, n_one, r_one, w_inner, w_outer, vectors, after):
    rows, width = d_outer.shape
    hidden_units = w_inner.shape[1]

    def kernel(d_out, d_sec, slope_ref, n_ref, r_ref, wi, wu, vec, d_in, d_first, d_attn, sums):
        d_first[...] = d_sec[...]
        for cut in range(0, hidden_units, FF_CUT):
            grad = dot_nt(d_out[...], wu[cut : cut + FF_CUT, :])
            grad = (grad * slope_ref[:, cut : cut + FF_CUT]).astype(BF)
            d_in[:, cut : cut + FF_CUT] = grad
            d_first[...] += dot_nt(grad, wi[:, cut : cut + FF_CUT])
        d_hidden = d_first[...]
        n = n_ref[...]
        sums[0:1, :] = jnp.sum(d_hidden * n, axis=0, keepdims=True)
        sums[1:2, :] = jnp.sum(d_hidden, axis=0, keepdims=True)
        first = normal_back(d_hidden * vec[0:1, :], n, r_ref[:, 0:1])
        d_first[...] = first
        d_attn[...] = first.astype(BF)

    return launch(
        kernel,
        (d_outer, d_second, slope, n_one, r_one, w_inner, w_outer, vectors),
        [vmem()] * 8,
        "feed_back",
        10,
        (
            like((rows, hidden_units), BF),
            like((rows, width), F32),
            like((rows, width), BF),
            like((2, width), F32),
        ),
        after=after,
    )


def attn_back(
    d_attn, probs, query, keys_all, values_all, w_out, query_at, key_at, first_pair, pairs, name, after
):
    rows, width = d_attn.shape
    columns = pairs * LANES
    head_count, _, keys = probs.shape
    half_span = REL // 2

    def kernel(*refs):
        d_at, p_ref, q_ref, k_ref, v_ref, wo, q_at, k_at = refs[:8]
        dq_ref, dk_ref, dv_ref, tables = refs[8:12]
        d_heads, heads_t, q_t, line_idx, key_hots, line_hots, row_hots, line_rows, rolls = refs[12:]
        base = first_pair * LANES
        grad = dot_nt(d_at[...], wo[base : base + columns, :])
        d_heads[...] = grad.astype(BF)
        heads_t[...] = grad.T.astype(BF)
        q_t[...] = q_ref[:, base : base + columns].astype(F32).T.astype(BF)
        line_idx[...] = line_index(q_at, k_at)
        lane = lax.broadcasted_iota(I32, (rows, LANES), 1)
        sub = lax.broadcasted_iota(I32, (LANES, keys), 0)
        place = jnp.where(sub < BOXES, k_at[2:3, :], k_at[3:4, :])
        key_hots[0:LANES] = ((sub & (BOXES - 1)) == place).astype(F32).astype(BF)
        key_hots[LANES:] = (sub == k_at[0:1, :]).astype(F32).astype(BF)
        line_hots[...] = (sub == (k_at[1:2, :] & (LANES - 1))).astype(F32).astype(BF)
        place = jnp.where(lane < BOXES, q_at[:, 2:3], q_at[:, 3:4])
        row_hots[...] = ((BOXES - 1 - (lane & (BOXES - 1))) == place).astype(F32).T.astype(BF)
        line_rows[...] = (
            ((LANES - 1 - lane) == (q_at[:, 1:2] & (LANES - 1))).astype(F32).T.astype(BF)
        )
        region_hot = (lane == q_at[:, 0:1]).astype(F32)
        tables[...] = jnp.zeros_like(tables)
        rolls[...] = jnp.zeros_like(rolls)
        square_row = lax.broadcasted_iota(I32, (LANES, LANES), 0)
        square_lane = lax.broadcasted_iota(I32, (LANES, LANES), 1)
        one_lane = lax.broadcasted_iota(I32, (1, LANES), 1)
        def rolled(square):
            return jnp.sum(
                pltpu.roll(square, 0, 1, stride=1, stride_axis=0), axis=0, keepdims=True
            )

        def pair(at, carry):
            col = pl.ds(pl.multiple_of(at * LANES, LANES), LANES)
            key_col = pl.ds(pl.multiple_of(base + at * LANES, LANES), LANES)
            d_pair, k_pair, v_pair = d_heads[:, col], k_ref[:, key_col], v_ref[:, key_col]
            back = []
            for half in range(2):
                head = 2 * (first_pair + at) + half
                own = pl.ds(pl.multiple_of(at * LANES + 64 * half, 64), 64)
                mine = (lane < 64) if half == 0 else (lane >= 64)
                d_one = jnp.where(mine, d_pair, jnp.zeros_like(d_pair))
                d_probs = dot_nt(d_one, v_pair)
                low_probs = p_ref[head]
                p_one = low_probs.astype(F32)
                row_dot = jnp.sum(p_one * d_probs, axis=1, keepdims=True)
                d_score = p_one * (d_probs - row_dot)
                low_score = d_score.astype(BF)
                back.append(dot_nn(low_score, k_pair))
                dk_ref[own, :] = dot_nn(q_t[own, :], low_score).astype(BF)
                dv_ref[own, :] = dot_nn(heads_t[own, :], low_probs).astype(BF)
                at_keys = dot_nt(low_score, key_hots[...])
                in_region = all_sum(at_keys[:, LANES:] * region_hot)
                boxes = at_keys[:, :LANES]
                whole = all_sum(jnp.where(lane < BOXES, boxes, 0.0))
                high, low = two_parts(boxes)
                square = dot_nn(row_hots[...], high) + dot_nn(row_hots[...], low)
                horiz = rolled(jnp.where((square_row < 64) & (square_lane < 64), square, 0.0))
                vert = pltpu.roll(
                    jnp.where((square_row >= 64) & (square_lane >= 64), square, 0.0),
                    64,
                    1,
                    stride=1,
                    stride_axis=0,
                )
                vert = jnp.sum(vert, axis=0, keepdims=True)
                near = line_idx[...] & (REL - 1)
                wide = low_score.astype(F32)
                inside = jnp.where((near > 0) & (near < REL - 1), wide, 0.0).astype(BF)
                before = all_sum(jnp.where(near == 0, wide, 0.0))
                high, low = two_parts(dot_nt(inside, line_hots[...]))
                square = dot_nn(line_rows[...], high) + dot_nn(line_rows[...], low)
                line = rolled(square)
                within = all_sum(square)
                rolls[0, pl.ds(head, 1), :] = horiz
                rolls[1, pl.ds(head, 1), :] = vert
                rolls[2, pl.ds(head, 1), :] = line
                row = jnp.where(one_lane == 0, before, 0.0)
                row = row + jnp.where(one_lane == REL - 1, whole - before - within, 0.0)
                row = row + jnp.where(one_lane == 3 * REL, in_region, 0.0)
                tables[pl.ds(head, 1), :] = row
            dq_ref[:, col] = (jnp.where(lane < 64, back[0], back[1]) * 0.125).astype(BF)
            return carry

        lax.fori_loop(0, pairs, pair, 0)
        bucket = square_lane & (REL - 1)

        def from_distance(distance):
            return jnp.clip(distance, -half_span, half_span - 1) + half_span

        horiz_map = (
            (from_distance(square_row - (BOXES - 1)) == bucket)
            & (square_lane >= REL)
            & (square_lane < 2 * REL)
        ).astype(F32)
        around = jnp.where(square_row < BOXES, square_row + 1, square_row + 1 - LANES)
        vert_map = (
            (from_distance(around) == bucket)
            & (square_lane >= 2 * REL)
            & (square_lane < 3 * REL)
        ).astype(F32)
        line_map = ((from_distance(around) == bucket) & (square_lane < REL)).astype(F32)

        def exact(left, right):
            return lax.dot_general(
                left,
                right,
                (((1,), (0,)), ((), ())),
                precision=lax.Precision.HIGHEST,
                preferred_element_type=F32,
            )

        tables[...] += (
            exact(rolls[0], horiz_map) + exact(rolls[1], vert_map) + exact(rolls[2], line_map)
        )

    return launch(
        kernel,
        (d_attn, probs, query, keys_all, values_all, w_out, query_at, key_at),
        [vmem()] * 8,
        name,
        8,
        (
            like((rows, columns), BF),
            like((columns, keys), BF),
            like((columns, keys), BF),
            like((16, LANES), F32),
        ),
        [
            pltpu.VMEM((rows, columns), BF),
            pltpu.VMEM((columns, rows), BF),
            pltpu.VMEM((columns, rows), BF),
            pltpu.VMEM((rows, keys), I32),
            pltpu.VMEM((2 * LANES, keys), BF),
            pltpu.VMEM((LANES, keys), BF),
            pltpu.VMEM((LANES, rows), BF),
            pltpu.VMEM((LANES, rows), BF),
            pltpu.VMEM((3, 16, LANES), F32),
        ],
        after,
    )


def rows_back(d_first, parts, weights, shards, after):
    rows, width = d_first.shape

    def kernel(*refs):
        first, wq, wk, wv = refs[:4]
        part_refs = refs[4 : 4 + 3 * len(parts)]
        own, *sent = refs[4 + 3 * len(parts) :]
        for at in range(shards - 1, -1, -1):
            cut = slice(at * rows, (at + 1) * rows)
            total, place = None, 0
            for group in range(len(parts)):
                _, dk, dv = part_refs[3 * group : 3 * group + 3]
                col = slice(place, place + dk.shape[0])
                value = dot_nn(wk[:, col], dk[:, cut]) + dot_nn(wv[:, col], dv[:, cut])
                total = value if total is None else total + value
                place += dk.shape[0]
            if at:
                sent[at - 1][...] = total.T.astype(BF)
                continue
            result, place = first[...] + total.T, 0
            for group in range(len(parts)):
                dq = part_refs[3 * group]
                col = slice(place, place + dq.shape[1])
                result = result + dot_nt(dq[...], wq[:, col])
                place += dq.shape[1]
            own[...] = result

    flat = [array for part in parts for array in part]
    return launch(
        kernel,
        (d_first, *weights, *flat),
        [vmem()] * (4 + len(flat)),
        "rows_back",
        8,
        (like((rows, width), F32),) + (like((rows, width), BF),) * (shards - 1),
        after=after,
    )


def swap(array_in, axis_name, flip):
    size = lax.axis_size(axis_name)
    return lax.ppermute(array_in, axis_name, [(at, at ^ flip) for at in range(size)])


def tok_shards(array_in):
    return [array_in] + [swap(array_in, "tok", step) for step in range(1, lax.axis_size("tok"))]


def xor_terms(groups, name, after=()):
    pages = lax.axis_size("page")
    page_index = lax.axis_index("page")
    width = groups[0][0].shape[1]
    rows = width // pages
    cols = [right.shape[1] if form == "nn" else right.shape[0] for _, right, form in groups]
    if rows % 16:
        whole = jnp.concatenate(
            [
                lax.dot_general(
                    left,
                    right,
                    (((0,), (0 if form == "nn" else 1,)), ((), ())),
                    preferred_element_type=F32,
                ).astype(BF)
                for left, right, form in groups
            ],
            1,
        ).reshape(pages, rows, -1)
        order = page_index ^ jnp.arange(pages)
        whole = jnp.take(whole, order, axis=0)
        return whole[0::2], whole[1::2]
    lefts, which = [], []
    for left, _, _ in groups:
        found = [at for at, item in enumerate(lefts) if item is left]
        which.append(found[0] if found else len(lefts))
        if not found:
            lefts.append(left)

    def kernel(page_ref, *refs):
        left_refs = refs[: len(lefts)]
        right_refs = refs[len(lefts) : len(lefts) + len(groups)]
        keep, send = refs[len(lefts) + len(groups) : len(lefts) + len(groups) + 2]
        turned = refs[len(lefts) + len(groups) + 2 :][: len(lefts)]
        picked = refs[2 * len(lefts) + len(groups) + 2 :]
        for left_ref, turned_ref in zip(left_refs, turned):
            turned_ref[...] = (
                left_ref[...].astype(F32).T.astype(BF).reshape(pages, rows, left_ref.shape[0])
            )
        page = page_ref[0]
        for odd, out in ((1, send), (0, keep)):
            for at, turned_ref in enumerate(turned):
                for step in range(pages // 2):
                    picked[at][step * rows : (step + 1) * rows] = turned_ref[
                        page ^ (2 * step + odd)
                    ]
            place = 0
            for at_left, right_ref, (_, _, form), count in zip(which, right_refs, groups, cols):
                for cut in range(0, count, 256):
                    end = min(cut + 256, count)
                    if form == "nn":
                        value = dot_nn(picked[at_left][...], right_ref[:, cut:end])
                    else:
                        value = dot_nt(picked[at_left][...], right_ref[cut:end, :])
                    out[:, :, place + cut : place + end] = value.astype(BF).reshape(
                        pages // 2, rows, end - cut
                    )
                place += count

    out = like((pages // 2, rows, sum(cols)), BF)
    return launch(
        kernel,
        (
            page_index.reshape(1).astype(I32),
            *lefts,
            *[right for _, right, _ in groups],
        ),
        [smem()] + [vmem()] * (len(lefts) + len(groups)),
        name,
        10,
        (out, out),
        [pltpu.VMEM((pages, rows, left.shape[0]), BF) for left in lefts]
        + [pltpu.VMEM((pages // 2 * rows, left.shape[0]), BF) for left in lefts],
        after,
    )


def split_sum(pairs, picks, name, after=()):
    def kernel(*refs):
        ins, outs = refs[: 2 * len(pairs)], refs[2 * len(pairs) :]
        for out, (pair, items, first, count) in zip(outs, picks):
            for at, item in enumerate(items):
                cut = slice(first, first + count)
                out[at] = ins[2 * pair][item, :, cut] + ins[2 * pair + 1][item, :, cut]

    rows = pairs[0][0].shape[1]
    return launch(
        kernel,
        [array for pair in pairs for array in pair],
        [vmem()] * (2 * len(pairs)),
        name,
        4,
        tuple(like((len(items), rows, count), BF) for _, items, _, count in picks),
        after=after,
    )


def tok_split(pairs, name, after=()):
    toks = lax.axis_size("tok")
    rows, cols = pairs[0][0].shape[1:]
    share = rows // toks
    arrays = [array.reshape(toks, share, cols) for pair in pairs for array in pair]

    def kernel(tok_ref, *refs):
        ins, outs = refs[: len(arrays)], refs[len(arrays) :]
        for step in range(toks):
            at = tok_ref[0] ^ step
            for pair in range(len(pairs)):
                value = ins[2 * pair][at].astype(F32) + ins[2 * pair + 1][at].astype(F32)
                out = outs[step]
                out[:, pair * cols : (pair + 1) * cols] = value.astype(out.dtype)

    full = (share, cols * len(pairs))
    return launch(
        kernel,
        (lax.axis_index("tok").reshape(1).astype(I32), *arrays),
        [smem()] + [vmem()] * len(arrays),
        name,
        4,
        (like(full, F32),) + (like(full, BF),) * (toks - 1),
        after=after,
    )


class Reduction:
    def __init__(self, keep, send, name):
        self.name = name
        self.pairs = [(keep, swap(send, "page", 1))]
        bits = [1 << at for at in range(1, lax.axis_size("page").bit_length() - 1)]
        self.orders = [bits, bits[::-1]]
        self.items = [list(range(0, lax.axis_size("page"), 2))] * 2

    def step(self, after=()):
        at_step = len(self.orders[0])
        cols = self.pairs[0][0].shape[2]
        first = len(self.pairs) == 1
        width = cols // 2 if first else cols
        picks, kept_items = [], []
        for half in range(2):
            bit = self.orders[half][0]
            items = self.items[half]
            where = (0, half * width) if first else (half, 0)
            for wanted in (bit, 0):
                chosen = [at for at, item in enumerate(items) if item & bit == wanted]
                picks.append((where[0], chosen, where[1], width))
            kept_items.append([item for item in items if not item & bit])
        outs = split_sum(self.pairs, picks, f"{self.name}_sum{at_step}", after)
        self.last = outs[-1]
        self.pairs = [
            (outs[2 * half + 1], swap(outs[2 * half], "page", self.orders[half][0]))
            for half in range(2)
        ]
        self.items = kept_items
        self.orders = [order[1:] for order in self.orders]

    def to_tok(self, after=()):
        while self.orders[0]:
            self.step(after)
        own, *sent = tok_split(self.pairs, f"{self.name}_tok", after)
        self.last = own
        self.shares = [own] + [swap(piece, "tok", at + 1) for at, piece in enumerate(sent)]

    def result(self):
        total = self.shares[0]
        for piece in self.shares[1:]:
            total = total + piece.astype(F32)
        return total


def sum_all(vector):
    bit = 1
    while bit < lax.axis_size("page"):
        vector = vector + swap(vector, "page", bit)
        bit *= 2
    bit = 1
    while bit < lax.axis_size("tok"):
        vector = vector + swap(vector, "tok", bit)
        bit *= 2
    return vector


def on_device(
    tokens,
    w_query,
    w_key,
    w_value,
    w_out,
    w_inner,
    w_outer,
    gain_one,
    shift_one,
    gain_two,
    shift_two,
    table_line,
    table_horiz,
    table_vert,
    region_weight,
    region_ids,
    line_pos,
    box_horiz,
    box_vert,
    cotangent,
):
    row_count, width = tokens.shape
    shards = lax.axis_size("tok")
    rows = -(-(row_count + 2) // 16) * 16

    def padded(array_in):
        return jnp.pad(array_in, ((0, rows - row_count), (0, 0)))

    def spread(*lines):
        return jnp.concatenate(
            [jnp.pad(line, (0, 256 - row_count)) for line in lines]
            + [jnp.zeros(width - 256 * len(lines), I32)]
        )

    info = jnp.stack(
        [spread(region_ids, line_pos // 32, line_pos % 32), spread(box_horiz, box_vert)]
    ).astype(BF)
    padded_tokens = jnp.concatenate(
        [tokens, jnp.zeros((rows - row_count - 2, width), BF), info], 0
    )
    token_shards = tok_shards(padded_tokens)
    places = jnp.stack([region_ids, line_pos, box_horiz, box_vert], 1)
    query_at = jnp.pad(places, ((0, rows - row_count), (0, 4)))
    line_table = jnp.concatenate(
        [
            table_line,
            table_line + region_weight[:, None],
            jnp.full((table_line.shape[0], LANES - 2 * REL), NEG, F32),
        ],
        1,
    )
    box_table = jnp.pad(
        jnp.concatenate([table_horiz, table_vert], 1), ((0, 0), (0, LANES - 2 * REL))
    )
    vectors = jnp.stack([gain_one, shift_one, gain_two, shift_two], 0)

    mix, query, keys_all, values_all, tokens_all, probs, key_at = attn_forward(
        token_shards, row_count, w_query, w_key, w_value, line_table, box_table, query_at
    )
    block, hidden, n_one, r_one, active, slope, d_second, d_outer, sums_two = feed_forward(
        mix, padded_tokens, w_out, w_inner, w_outer, vectors, padded(cotangent)
    )
    terms = xor_terms([(active, d_outer, "nn")], "outer_terms")
    outer = Reduction(*terms, "outer")
    d_inner, d_first, d_attn, sums_one = feed_back(
        d_outer, d_second, slope, n_one, r_one, w_inner, w_outer, vectors, (terms[0],)
    )
    outer.step((d_attn,))
    terms = xor_terms(
        [(hidden, d_inner, "nn"), (mix, d_attn, "nn")], "inner_terms", (outer.last,)
    )
    inner = Reduction(*terms, "inner")
    half_pairs = width // LANES // 2
    parts, table_parts, done = [], [], terms[0]
    for group in range(2):
        *part, table_part = attn_back(
            d_attn,
            probs,
            query,
            keys_all,
            values_all,
            w_out,
            query_at,
            key_at,
            group * half_pairs,
            half_pairs,
            f"attn_back{group}",
            (done,),
        )
        parts.append(part)
        table_parts.append(table_part)
        if group == 0:
            inner.step((table_part,))
            outer.step((inner.last,))
            done = outer.last
    terms = xor_terms(
        [(padded_tokens, part[0], "nn") for part in parts]
        + [(tokens_all, part[1], "nt") for part in parts]
        + [(tokens_all, part[2], "nt") for part in parts],
        "attn_terms",
    )
    attn = Reduction(*terms, "attn")
    d_own, *sent = rows_back(
        d_first, parts, (w_query, w_key, w_value), shards, (terms[0],)
    )
    inner.step((d_own,))
    attn.step((inner.last,))
    outer.to_tok((attn.last,))
    back = [swap(piece, "tok", at + 1) for at, piece in enumerate(sent)]
    small = jnp.concatenate(
        [
            sums_one.reshape(-1, LANES),
            sums_two.reshape(-1, LANES),
            table_parts[0] + table_parts[1],
        ],
        0,
    )
    small = sum_all(small)
    attn.step((outer.last,))
    inner.to_tok((attn.last,))
    attn.to_tok((inner.last,))
    for piece in back:
        d_own = d_own + piece.astype(F32)
    d_tokens = d_own[:row_count].astype(BF)
    vector_rows = width // LANES
    vector_sums = small[: 4 * vector_rows].reshape(4, width)
    tables = small[4 * vector_rows :][: table_line.shape[0]]
    grad_attn = attn.result()
    grad_attn = [grad_attn[:, at * width : (at + 1) * width] for at in range(3)]
    grad_inner = inner.result()
    units = w_inner.shape[1]
    return (
        block[:row_count],
        d_tokens,
        *grad_attn,
        grad_inner[:, units:],
        grad_inner[:, :units],
        outer.result(),
        vector_sums[0],
        vector_sums[1],
        vector_sums[2],
        vector_sums[3],
        tables[:, 0:REL],
        tables[:, REL : 2 * REL],
        tables[:, 2 * REL : 3 * REL],
        tables[:, 3 * REL],
    )


def solution(mesh):
    placed = (
        P(("page", "tok"), None),
        P(),
        P(),
        P(),
        P(),
        P(),
        P(),
        P(),
        P(),
        P(),
        P(),
        P(),
        P(),
        P(),
        P(),
        P(("page", "tok")),
        P(("page", "tok")),
        P(("page", "tok")),
        P(("page", "tok")),
        P(("page", "tok"), None),
    )
    return jax.shard_map(
        on_device,
        mesh=mesh,
        in_specs=placed,
        out_specs=(
            P(("page", "tok"), None),
            P(("page", "tok"), None),
            P(("page", "tok"), None),
            P(("page", "tok"), None),
            P(("page", "tok"), None),
            P(("page", "tok"), None),
            P(("page", "tok"), None),
            P(("page", "tok"), None),
            P(),
            P(),
            P(),
            P(),
            P(),
            P(),
            P(),
            P(),
        ),
        check_vma=False,
    )
```

```python
import math

import jax
import jax.numpy as jnp
from jax import lax
from jax.experimental import pallas as pl
from jax.experimental.pallas import tpu as pltpu
from jax.sharding import PartitionSpec as P

REL = 32
BOXES = 64
BF = jnp.bfloat16
F32 = jnp.float32
I32 = jnp.int32
NEG = -1e30
LANES = 128
MIB = 2**20


def vmem():
    return pl.BlockSpec(memory_space=pltpu.VMEM)


def like(shape, kind):
    return jax.ShapeDtypeStruct(shape, kind)


class Later:
    def __init__(self, stage, index):
        self.stage, self.index = stage, index
        self.shape, self.dtype = stage.outs[index].shape, stage.outs[index].dtype


class Stage:
    def __init__(self, body, operands, specs, outs, scratch=()):
        self.body, self.operands, self.specs = body, list(operands), list(specs)
        self.outs, self.scratch = list(outs), list(scratch)
        self.results = [Later(self, index) for index in range(len(self.outs))]


def run(stages, name, limit, after=()):
    arrays, specs, place = [], [], {}
    for stage in stages:
        for operand, spec in zip(stage.operands, stage.specs):
            if not isinstance(operand, Later) and id(operand) not in place:
                place[id(operand)] = len(arrays)
                arrays.append(operand)
                specs.append(spec)
    out_shape = [out for stage in stages for out in stage.outs]

    def kernel(*refs):
        ins = refs[: len(arrays)]
        outs = list(refs[len(arrays) + len(after) :][: len(out_shape)])
        scratch = list(refs[len(arrays) + len(after) + len(out_shape) :])
        given = {}
        for stage in stages:
            own = [outs.pop(0) for _ in stage.outs]
            spare = [scratch.pop(0) for _ in stage.scratch]
            given[id(stage)] = own
            read = [
                given[id(item.stage)][item.index]
                if isinstance(item, Later)
                else ins[place[id(item)]]
                for item in stage.operands
            ]
            stage.body(*read, *own, *spare)

    return pl.pallas_call(
        kernel,
        out_shape=tuple(out_shape),
        in_specs=specs + [pl.BlockSpec(memory_space=pl.ANY)] * len(after),
        out_specs=[vmem()] * len(out_shape),
        scratch_shapes=[item for stage in stages for item in stage.scratch],
        compiler_params=pltpu.CompilerParams(vmem_limit_bytes=limit * MIB),
        name=name,
    )(*arrays, *after)


def dot_nn(left, right):
    return lax.dot_general(left, right, (((1,), (0,)), ((), ())), preferred_element_type=F32)


def dot_nt(left, right):
    return lax.dot_general(left, right, (((1,), (1,)), ((), ())), preferred_element_type=F32)


def look(table_row, index):
    return jnp.take_along_axis(jnp.broadcast_to(table_row, index.shape), index, axis=1)


def two_parts(value):
    high = value.astype(BF)
    return high, (value - high.astype(F32)).astype(BF)


def key_places(info, shard, rows, keys):
    pieces = []
    for at in range(3):
        wide = jnp.concatenate(
            [info[:, at * 256 : (at + 1) * 256], jnp.zeros((16, keys - 256), F32)], 1
        )
        pieces.append(pltpu.roll(wide, shard * rows, 1) if shard else wide)
    return pieces


def line_index(query_at, key_at):
    bucket = jnp.clip(key_at[1:2, :] - query_at[:, 1:2], -(REL // 2), REL // 2 - 1) + REL // 2
    same = jnp.where(query_at[:, 0:1] == key_at[0:1, :], REL, 0)
    return jnp.where(key_at[4:5, :] > 0, bucket + same, 2 * REL)


def attn_forward(token_shards, row_count, weights, line_table, box_table, query_at):
    rows, width = token_shards[0].shape
    head_count = line_table.shape[0]
    shards = len(token_shards)
    keys = -(-rows * shards // LANES) * LANES

    def kernel(*refs):
        tok_refs = refs[:shards]
        wk, wv, wq, line_ref, box_ref, q_at = refs[shards : shards + 6]
        mix_ref, q_ref, k_ref, v_ref, x_ref, p_ref, k_at = refs[shards + 6 : shards + 13]
        line_idx, box_idx, hots = refs[shards + 13 :]
        places = [jnp.zeros((16, keys), F32)] * 3
        for at in range(shards):
            info = tok_refs[at][rows - 16 :, :].astype(F32)
            places = [
                left + right for left, right in zip(places, key_places(info, at, rows, keys))
            ]
        lane = lax.broadcasted_iota(I32, (1, keys), 1)
        live = jnp.zeros((1, keys), I32)
        for at in range(shards):
            inside = (lane >= at * rows) & (lane < at * rows + row_count)
            live = jnp.where(inside, 1, live)
        k_at[...] = jnp.zeros_like(k_at)
        k_at[0:1] = places[0][14:15].astype(I32)
        k_at[1:2] = (places[1][14:15] * 32.0 + places[2][14:15]).astype(I32)
        k_at[2:3] = places[0][15:16].astype(I32)
        k_at[3:4] = places[1][15:16].astype(I32)
        k_at[4:5] = live
        for at in range(shards):
            x_ref[at * rows : (at + 1) * rows] = tok_refs[at][...]
        if keys > shards * rows:
            x_ref[shards * rows :] = jnp.zeros((keys - shards * rows, width), BF)
        k_ref[...] = dot_nn(x_ref[...], wk[...]).astype(BF)
        v_ref[...] = dot_nn(x_ref[...], wv[...]).astype(BF)
        q_ref[...] = (dot_nn(tok_refs[0][...], wq[...]) * 0.125).astype(BF)
        line_idx[...] = line_index(q_at, k_at)
        lane = lax.broadcasted_iota(I32, (rows, LANES), 1)
        place = jnp.where(lane < BOXES, q_at[:, 2:3], q_at[:, 3:4])
        bucket = jnp.clip((lane & (BOXES - 1)) - place, -(REL // 2), REL // 2 - 1) + REL // 2
        box_idx[...] = bucket + jnp.where(lane < BOXES, 0, REL)
        sub = lax.broadcasted_iota(I32, (LANES, keys), 0)
        place = jnp.where(sub < BOXES, k_at[2:3, :], k_at[3:4, :])
        hot = ((sub & (BOXES - 1)) == place).astype(F32).astype(BF)
        hots[0:LANES] = hot
        hots[LANES:] = hot

        def pair(at, carry):
            col = pl.ds(pl.multiple_of(at * LANES, LANES), LANES)
            q_pair, k_pair, v_pair = q_ref[:, col], k_ref[:, col], v_ref[:, col]
            mixed = []
            for half in range(2):
                head = 2 * at + half
                mine = (lane < 64) if half == 0 else (lane >= 64)
                q_one = jnp.where(mine, q_pair, jnp.zeros_like(q_pair))
                high, low = two_parts(look(box_ref[pl.ds(head, 1), :], box_idx[...]))
                score = dot_nt(q_one, k_pair) + dot_nn(jnp.concatenate([high, low], 1), hots[...])
                line_row = line_ref[pl.ds(head, 1), :]
                score = score + jnp.concatenate(
                    [
                        look(line_row, line_idx[:, cut : cut + LANES])
                        for cut in range(0, keys, LANES)
                    ],
                    1,
                )
                grown = jnp.exp(score - jnp.max(score, axis=1, keepdims=True))
                probs = grown * (1.0 / jnp.sum(grown, axis=1, keepdims=True))
                low_probs = probs.astype(BF)
                p_ref[pl.ds(head, 1)] = low_probs[None]
                mixed.append(dot_nn(low_probs, v_pair))
            mix_ref[:, col] = jnp.where(lane < 64, mixed[0], mixed[1]).astype(BF)
            return carry

        lax.fori_loop(0, width // LANES, pair, 0)

    return Stage(
        kernel,
        (*token_shards, *weights, line_table, box_table, query_at),
        [vmem()] * (shards + 6),
        (
            like((rows, width), BF),
            like((rows, width), BF),
            like((keys, width), BF),
            like((keys, width), BF),
            like((keys, width), BF),
            like((head_count, rows, keys), BF),
            like((8, keys), I32),
        ),
        [
            pltpu.VMEM((rows, keys), I32),
            pltpu.VMEM((rows, LANES), I32),
            pltpu.VMEM((2 * LANES, keys), BF),
        ],
    )


def row_mean(value):
    return jnp.mean(value, axis=1, keepdims=True)


def all_sum(value):
    return jnp.sum(jnp.sum(value, axis=1, keepdims=True), axis=0, keepdims=True)


def normal(value):
    centered = value - row_mean(value)
    scale = lax.rsqrt(row_mean(centered * centered) + 1e-05)
    return centered * scale, scale


def normal_back(d_normal, n, scale):
    return scale * (d_normal - row_mean(d_normal) - n * row_mean(d_normal * n))


FF_CUT = 512


def feed_forward(mix, tokens, row_count, w_out, w_inner, w_outer, vectors, cotangent):
    rows, width = tokens.shape

    hidden_units = w_inner.shape[1]

    def kernel(mix_ref, tok, wo, wi, wu, vec, cot, *outs):
        block, hid, n_one, r_one, act, slope, d_sec, d_out, sums, total = outs
        n, r = normal(tok[...].astype(F32) + dot_nn(mix_ref[...], wo[...]))
        n_one[...] = n
        r_one[...] = jnp.broadcast_to(r, r_one.shape)
        hidden = n * vec[0:1, :] + vec[1:2, :]
        hid[...] = hidden.astype(BF)
        total[...] = hidden
        for cut in range(0, hidden_units, FF_CUT):
            inner = dot_nn(hid[...], wi[:, cut : cut + FF_CUT])
            upper = 0.5 + 0.5 * lax.erf(inner * (0.5**0.5))
            active = (inner * upper).astype(BF)
            act[:, cut : cut + FF_CUT] = active
            bell = jnp.exp(-0.5 * inner * inner) * (2.0 * math.pi) ** -0.5
            slope[:, cut : cut + FF_CUT] = upper + inner * bell
            total[...] += dot_nn(active, wu[cut : cut + FF_CUT, :])
        n, r = normal(total[...])
        block[...] = (n * vec[2:3, :] + vec[3:4, :])[:row_count].astype(BF)
        grad = cot[...].astype(F32)
        sums[0:1, :] = jnp.sum(grad * n, axis=0, keepdims=True)
        sums[1:2, :] = jnp.sum(grad, axis=0, keepdims=True)
        second = normal_back(grad * vec[2:3, :], n, r)
        d_sec[...] = second
        d_out[...] = second.astype(BF)

    return Stage(
        kernel,
        (mix, tokens, w_out, w_inner, w_outer, vectors, cotangent),
        [vmem()] * 7,
        (
            like((row_count, width), BF),
            like((rows, width), BF),
            like((rows, width), F32),
            like((rows, LANES), F32),
            like((rows, hidden_units), BF),
            like((rows, hidden_units), F32),
            like((rows, width), F32),
            like((rows, width), BF),
            like((2, width), F32),
        ),
        [pltpu.VMEM((rows, width), F32)],
    )


def feed_back(d_outer, d_second, slope, n_one, r_one, w_inner, w_outer, w_out, vectors):
    rows, width = d_outer.shape
    hidden_units = w_inner.shape[1]

    def kernel(*refs):
        d_out, d_sec, slope_ref, n_ref, r_ref, wi, wu, wo, vec = refs[:9]
        d_in, d_first, d_attn, sums, d_heads = refs[9:]
        d_first[...] = d_sec[...]
        for cut in range(0, hidden_units, FF_CUT):
            grad = dot_nt(d_out[...], wu[cut : cut + FF_CUT, :])
            grad = (grad * slope_ref[:, cut : cut + FF_CUT]).astype(BF)
            d_in[:, cut : cut + FF_CUT] = grad
            d_first[...] += dot_nt(grad, wi[:, cut : cut + FF_CUT])
        d_hidden = d_first[...]
        n = n_ref[...]
        sums[0:1, :] = jnp.sum(d_hidden * n, axis=0, keepdims=True)
        sums[1:2, :] = jnp.sum(d_hidden, axis=0, keepdims=True)
        first = normal_back(d_hidden * vec[0:1, :], n, r_ref[:, 0:1])
        d_first[...] = first
        d_attn[...] = first.astype(BF)
        d_heads[...] = dot_nt(d_attn[...], wo[...]).astype(BF)

    return Stage(
        kernel,
        (d_outer, d_second, slope, n_one, r_one, w_inner, w_outer, w_out, vectors),
        [vmem()] * 9,
        (
            like((rows, hidden_units), BF),
            like((rows, width), F32),
            like((rows, width), BF),
            like((2, width), F32),
            like((rows, width), BF),
        ),
    )


def attn_back(
    d_heads, probs, query, keys_all, values_all, query_at, key_at, first_pair, pairs
):
    rows, width = d_heads.shape
    columns = pairs * LANES
    head_count, _, keys = probs.shape
    half_span = REL // 2

    def kernel(*refs):
        d_ref, p_ref, q_ref, k_ref, v_ref, q_at, k_at = refs[:7]
        dq_ref, dk_ref, dv_ref, tables = refs[7:11]
        heads_t, q_t, line_idx, key_hots, line_hots, row_hots, line_rows, rolls = refs[11:]
        base = first_pair * LANES
        heads_t[...] = d_ref[:, base : base + columns].astype(F32).T.astype(BF)
        q_t[...] = q_ref[:, base : base + columns].astype(F32).T.astype(BF)
        line_idx[...] = line_index(q_at, k_at)
        lane = lax.broadcasted_iota(I32, (rows, LANES), 1)
        sub = lax.broadcasted_iota(I32, (LANES, keys), 0)
        place = jnp.where(sub < BOXES, k_at[2:3, :], k_at[3:4, :])
        key_hots[0:LANES] = ((sub & (BOXES - 1)) == place).astype(F32).astype(BF)
        key_hots[LANES:] = (sub == k_at[0:1, :]).astype(F32).astype(BF)
        line_hots[...] = (sub == (k_at[1:2, :] & (LANES - 1))).astype(F32).astype(BF)
        place = jnp.where(lane < BOXES, q_at[:, 2:3], q_at[:, 3:4])
        row_hots[...] = ((BOXES - 1 - (lane & (BOXES - 1))) == place).astype(F32).T.astype(BF)
        line_rows[...] = (
            ((LANES - 1 - lane) == (q_at[:, 1:2] & (LANES - 1))).astype(F32).T.astype(BF)
        )
        region_hot = (lane == q_at[:, 0:1]).astype(F32)
        tables[...] = jnp.zeros_like(tables)
        rolls[...] = jnp.zeros_like(rolls)
        square_row = lax.broadcasted_iota(I32, (LANES, LANES), 0)
        square_lane = lax.broadcasted_iota(I32, (LANES, LANES), 1)
        one_lane = lax.broadcasted_iota(I32, (1, LANES), 1)
        def rolled(square):
            return jnp.sum(
                pltpu.roll(square, 0, 1, stride=1, stride_axis=0), axis=0, keepdims=True
            )

        def pair(at, carry):
            col = pl.ds(pl.multiple_of(at * LANES, LANES), LANES)
            key_col = pl.ds(pl.multiple_of(base + at * LANES, LANES), LANES)
            d_pair, k_pair, v_pair = d_ref[:, key_col], k_ref[:, key_col], v_ref[:, key_col]
            back = []
            for half in range(2):
                head = 2 * (first_pair + at) + half
                own = pl.ds(pl.multiple_of(at * LANES + 64 * half, 64), 64)
                mine = (lane < 64) if half == 0 else (lane >= 64)
                d_one = jnp.where(mine, d_pair, jnp.zeros_like(d_pair))
                d_probs = dot_nt(d_one, v_pair)
                low_probs = p_ref[head]
                p_one = low_probs.astype(F32)
                row_dot = jnp.sum(p_one * d_probs, axis=1, keepdims=True)
                d_score = p_one * (d_probs - row_dot)
                low_score = d_score.astype(BF)
                back.append(dot_nn(low_score, k_pair))
                dk_ref[own, :] = dot_nn(q_t[own, :], low_score).astype(BF)
                dv_ref[own, :] = dot_nn(heads_t[own, :], low_probs).astype(BF)
                at_keys = dot_nt(low_score, key_hots[...])
                in_region = all_sum(at_keys[:, LANES:] * region_hot)
                boxes = at_keys[:, :LANES]
                whole = all_sum(jnp.where(lane < BOXES, boxes, 0.0))
                high, low = two_parts(boxes)
                square = dot_nn(row_hots[...], high) + dot_nn(row_hots[...], low)
                horiz = rolled(jnp.where((square_row < 64) & (square_lane < 64), square, 0.0))
                vert = pltpu.roll(
                    jnp.where((square_row >= 64) & (square_lane >= 64), square, 0.0),
                    64,
                    1,
                    stride=1,
                    stride_axis=0,
                )
                vert = jnp.sum(vert, axis=0, keepdims=True)
                near = line_idx[...] & (REL - 1)
                wide = low_score.astype(F32)
                inside = jnp.where((near > 0) & (near < REL - 1), wide, 0.0).astype(BF)
                before = all_sum(jnp.where(near == 0, wide, 0.0))
                high, low = two_parts(dot_nt(inside, line_hots[...]))
                square = dot_nn(line_rows[...], high) + dot_nn(line_rows[...], low)
                line = rolled(square)
                within = all_sum(square)
                rolls[0, pl.ds(head, 1), :] = horiz
                rolls[1, pl.ds(head, 1), :] = vert
                rolls[2, pl.ds(head, 1), :] = line
                row = jnp.where(one_lane == 0, before, 0.0)
                row = row + jnp.where(one_lane == REL - 1, whole - before - within, 0.0)
                row = row + jnp.where(one_lane == 3 * REL, in_region, 0.0)
                tables[pl.ds(head, 1), :] = row
            dq_ref[:, col] = (jnp.where(lane < 64, back[0], back[1]) * 0.125).astype(BF)
            return carry

        lax.fori_loop(0, pairs, pair, 0)
        bucket = square_lane & (REL - 1)

        def from_distance(distance):
            return jnp.clip(distance, -half_span, half_span - 1) + half_span

        horiz_map = (
            (from_distance(square_row - (BOXES - 1)) == bucket)
            & (square_lane >= REL)
            & (square_lane < 2 * REL)
        ).astype(F32)
        around = jnp.where(square_row < BOXES, square_row + 1, square_row + 1 - LANES)
        vert_map = (
            (from_distance(around) == bucket)
            & (square_lane >= 2 * REL)
            & (square_lane < 3 * REL)
        ).astype(F32)
        line_map = ((from_distance(around) == bucket) & (square_lane < REL)).astype(F32)

        def exact(left, right):
            return lax.dot_general(
                left,
                right,
                (((1,), (0,)), ((), ())),
                precision=lax.Precision.HIGHEST,
                preferred_element_type=F32,
            )

        tables[...] += (
            exact(rolls[0], horiz_map) + exact(rolls[1], vert_map) + exact(rolls[2], line_map)
        )

    return Stage(
        kernel,
        (d_heads, probs, query, keys_all, values_all, query_at, key_at),
        [vmem()] * 7,
        (
            like((rows, columns), BF),
            like((columns, keys), BF),
            like((columns, keys), BF),
            like((16, LANES), F32),
        ),
        [
            pltpu.VMEM((columns, rows), BF),
            pltpu.VMEM((columns, rows), BF),
            pltpu.VMEM((rows, keys), I32),
            pltpu.VMEM((2 * LANES, keys), BF),
            pltpu.VMEM((LANES, keys), BF),
            pltpu.VMEM((LANES, rows), BF),
            pltpu.VMEM((LANES, rows), BF),
            pltpu.VMEM((3, 16, LANES), F32),
        ],
    )


def fetch(weights):
    count = len(weights)

    def kernel(*refs):
        copies = [
            pltpu.make_async_copy(far, near, refs[-1].at[at])
            for at, (far, near) in enumerate(zip(refs[:count], refs[count:-1]))
        ]
        for copy in copies:
            copy.start()
        for copy in copies:
            copy.wait()

    return Stage(
        kernel,
        weights,
        [pl.BlockSpec(memory_space=pltpu.HBM)] * count,
        [like(weight.shape, BF) for weight in weights],
        [pltpu.SemaphoreType.DMA((count,))],
    )


def rows_back(d_first, parts, weights, shards):
    rows, width = d_first.shape

    def kernel(*refs):
        first, wq, wk, wv = refs[:4]
        part_refs = refs[4 : 4 + 3 * len(parts)]
        own, send, keep = refs[4 + 3 * len(parts) :]
        for at in range(shards - 1, -1, -1):
            cut = slice(at * rows, (at + 1) * rows)
            total, place = None, 0
            for group in range(len(parts)):
                _, dk, dv = part_refs[3 * group : 3 * group + 3]
                col = slice(place, place + dk.shape[0])
                value = dot_nn(wk[:, col], dk[:, cut]) + dot_nn(wv[:, col], dv[:, cut])
                total = value if total is None else total + value
                place += dk.shape[0]
            if at % 2:
                send[at // 2] = total.T.astype(BF)
                continue
            if at:
                keep[at // 2 - 1] = total.T.astype(BF)
                continue
            result, place = first[...] + total.T, 0
            for group in range(len(parts)):
                dq = part_refs[3 * group]
                col = slice(place, place + dq.shape[1])
                result = result + dot_nt(dq[...], wq[:, col])
                place += dq.shape[1]
            own[...] = result

    flat = [array for part in parts for array in part]
    return Stage(
        kernel,
        (d_first, *weights, *flat),
        [vmem()] * (4 + len(flat)),
        (
            like((rows, width), F32),
            like((shards // 2, rows, width), BF),
            like((shards // 2 - 1, rows, width), BF),
        ),
    )


def rows_step(own, keep, got):
    def kernel(own_ref, keep_ref, got_ref, out, send):
        out[...] = own_ref[...] + got_ref[0].astype(F32)
        send[...] = keep_ref[0] + got_ref[1]

    return Stage(kernel, (own, keep, got), [vmem()] * 3, (like(own.shape, F32), like(own.shape, BF)))


def rows_result(own, got, row_count):
    def kernel(own_ref, got_ref, out):
        out[...] = (own_ref[...] + got_ref[...].astype(F32))[:row_count].astype(BF)

    return Stage(kernel, (own, got), [vmem()] * 2, (like((row_count, own.shape[1]), BF),))


def pack(sums, tables):
    width = sums[0].shape[1]
    height = sum(item.shape[0] for item in sums) * width // LANES

    def kernel(*refs):
        out, place = refs[-1], 0
        for ref in refs[: len(sums)]:
            for row in range(ref.shape[0]):
                for cut in range(0, width, LANES):
                    out[place : place + 1] = ref[row : row + 1, cut : cut + LANES]
                    place += 1
        total = refs[len(sums)][...]
        for ref in refs[len(sums) + 1 : -1]:
            total = total + ref[...]
        out[place : place + total.shape[0]] = total
        out[place + total.shape[0] :] = jnp.zeros_like(out[place + total.shape[0] :])

    operands = (*sums, *tables)
    return Stage(
        kernel, operands, [vmem()] * len(operands), (like((-(-(height + tables[0].shape[0]) // 16) * 16, LANES), F32),)
    )


def swap(array_in, axis_name, flip):
    size = lax.axis_size(axis_name)
    return lax.ppermute(array_in, axis_name, [(at, at ^ flip) for at in range(size)])


def tok_shards(array_in):
    return [array_in] + [swap(array_in, "tok", step) for step in range(1, lax.axis_size("tok"))]


def two_halves(value):
    high, low = two_parts(value)
    return jnp.concatenate([high.astype(F32), low.astype(F32)], 0)


def whole_value(halves):
    return halves[: halves.shape[0] // 2] + halves[halves.shape[0] // 2 :]


def put_load(out, item, value):
    halves = two_halves(value)
    rows, cols = out.shape[1:]
    count = halves.shape[0] // rows
    for at in range(count):
        low = cols - (count - at) * LANES
        out[item, :, low : low + LANES] = halves[at * rows : (at + 1) * rows].astype(BF)


class Cut:
    def __init__(self, array, low, high):
        self.array, self.low, self.high = array, low, high


def cut_of(right, form):
    if isinstance(right, Cut):
        return right
    return Cut(right, 0, right.shape[form == "nn"])


def xor_terms(groups, cuts, load=None):
    pages = lax.axis_size("page")
    width = groups[0][0].shape[1]
    rows = width // pages
    rights = [cut_of(right, form) for _, right, form in groups]
    cols = [right.high - right.low for right in rights]
    lefts, which = [], []
    for left, _, _ in groups:
        found = [at for at, item in enumerate(lefts) if item is left]
        which.append(found[0] if found else len(lefts))
        if not found:
            lefts.append(left)

    def kernel(*refs):
        if load is not None:
            load_ref, refs = refs[0], refs[1:]
        left_refs = refs[: len(lefts)]
        right_refs = refs[len(lefts) : len(lefts) + len(groups)]
        keep, *sends = refs[len(lefts) + len(groups) :][: 1 + len(cuts)]
        rest = refs[1 + len(cuts) + len(lefts) + len(groups) :]
        turned, picked = rest[: len(lefts)], rest[len(lefts) :]
        for left_ref, turned_ref in zip(left_refs, turned):
            turned_ref[...] = (
                left_ref[...].astype(F32).T.astype(BF).reshape(pages, rows, left_ref.shape[0])
            )
        page = lax.axis_index("page")
        for odd in (1, 0):
            for at, turned_ref in enumerate(turned):
                for step in range(pages // 2):
                    picked[at][step * rows : (step + 1) * rows] = turned_ref[
                        page ^ (2 * step + odd)
                    ]
            place = 0
            outs = [out for out, count in zip(sends, cuts) for _ in range(count)]
            for at_left, right_ref, right, (_, _, form), count, out in zip(
                which, right_refs, rights, groups, cols, outs if odd else [keep] * len(groups)
            ):
                if odd and place and out is not last:
                    place = 0
                last = out
                for cut in range(0, count, 256):
                    end = min(cut + 256, count)
                    used = slice(right.low + cut, right.low + end)
                    if form == "nn":
                        value = dot_nn(picked[at_left][...], right_ref[:, used])
                    else:
                        value = dot_nt(picked[at_left][...], right_ref[used, :])
                    out[:, :, place + cut : place + end] = value.astype(BF).reshape(
                        pages // 2, rows, end - cut
                    )
                place += count
        if load is not None:
            put_load(sends[-1], 0, load_ref[...])

    sizes, first = [sum(cols)], 0
    for count in cuts:
        sizes.append(sum(cols[first : first + count]))
        first += count
    if load is not None:
        sizes[-1] += LANES
    extra = [] if load is None else [load]
    return Stage(
        kernel,
        (
            *extra,
            *lefts,
            *[right.array for right in rights],
        ),
        [vmem()] * (len(extra) + len(lefts) + len(groups)),
        [like((pages // 2, rows, size), BF) for size in sizes],
        [pltpu.VMEM((pages, rows, left.shape[0]), BF) for left in lefts]
        + [pltpu.VMEM((pages // 2 * rows, left.shape[0]), BF) for left in lefts],
    )


def plain_terms(groups):
    pages, parts = lax.axis_size("page"), []
    for left, right, form in groups:
        cut = cut_of(right, form)
        side = int(form == "nn")
        used = lax.slice_in_dim(cut.array, cut.low, cut.high, axis=side)
        part = lax.dot_general(
            left, used, (((0,), (1 - side,)), ((), ())), preferred_element_type=F32
        )
        parts.append(part.astype(BF))
    whole = jnp.concatenate(parts, 1)
    whole = whole.reshape(pages, whole.shape[0] // pages, whole.shape[1])
    whole = jnp.take(whole, lax.axis_index("page") ^ jnp.arange(pages), axis=0)
    return whole[0::2], [whole[1::2]]


def with_terms(stages, sums, name, limit, after=(), load=None, cuts=None):
    width, pages = sums[0][0][0].shape[1], lax.axis_size("page")
    if width // pages % 16:
        outs = run(stages, name, limit, after) if stages else ()
        order = [item for stage in stages for item in stage.results]

        def real(item):
            return outs[order.index(item)] if isinstance(item, Later) else item

        return [
            plain_terms([(real(left), real(right), form) for left, right, form in groups])
            for groups in sums
        ], outs
    last = [xor_terms(groups, cuts or [len(groups)], load) for groups in sums]
    outs = run([*stages, *last], name, limit, after)
    each = 1 + len(cuts or [0])
    count = len(outs) - each * len(sums)
    terms = [(outs[at], list(outs[at + 1 : at + each])) for at in range(count, len(outs), each)]
    return terms, outs[:count]


def plain_sum(pair):
    def kernel(left, right, out):
        out[...] = left[...] + right[...]

    return Stage(kernel, pair, [vmem()] * 2, (like(pair[0].shape, pair[0].dtype),))


class Rider:
    def __init__(self, vector, path):
        self.path = [("page", 1)] + path
        self.move(vector)

    def stage(self):
        return plain_sum(self.pair)

    def move(self, vector):
        self.pair = (vector, swap(vector, *self.path.pop(0)))


def add_columns(kept, got, at, low, high, kind):
    ends = set()
    for pieces in (kept, got):
        place = 0
        for piece in pieces:
            place += piece.shape[-1]
            ends.add(place)
    ends = sorted(end for end in ends if low < end < high) + [high]

    def read(pieces, first, last):
        place = 0
        for piece in pieces:
            if place <= first and last <= place + piece.shape[-1]:
                return piece[(*at, slice(None), slice(first - place, last - place))].astype(kind)
            place += piece.shape[-1]

    values, first = [], low
    for end in ends:
        values.append(read(kept, first, end) + read(got, first, end))
        first = end
    return values[0] if len(values) == 1 else jnp.concatenate(values, 1)


class Reduction:
    def __init__(self, terms, name, turn=False, tok_first=False):
        keep, sends = terms
        pages, toks = lax.axis_size("page"), lax.axis_size("tok")
        self.name, self.count, self.pages, self.toks = name, 0, pages, toks
        bits = [1 << at for at in range(1, pages.bit_length() - 1)]
        page_path = [("page", bit) for bit in (bits[::-1] if turn else bits)]
        tok_path = [("tok", 1 << at) for at in range(toks.bit_length() - 1)]
        self.path = tok_path + page_path if tok_first else page_path + tok_path
        self.labels, self.split = list(range(0, pages, 2)), False
        self.kept, self.got = [keep], [swap(piece, "page", 1) for piece in sends]

    def join(self, other):
        self.kept, self.got = self.kept + other.kept, self.got + other.got

    def step(self, after=(), rider=None, cuts=None):
        begun = self.count > 0
        self.halve(after, rider, cuts)
        while begun and self.path and self.path[0][0] == "page":
            self.halve(after, rider)

    def halve(self, after=(), rider=None, cuts=None):
        axis, bit = self.path.pop(0)
        flag = bit if axis == "page" else bit * self.pages
        first = axis == "tok" and not self.split
        arrays, toks = [*self.kept, *self.got], self.toks
        rows, cols = self.kept[0].shape[1], sum(array.shape[2] for array in self.kept)
        if first:
            rows //= toks
            arrays = [a.reshape(a.shape[0], toks, rows, a.shape[2]) for a in arrays]
            self.labels = [at + self.pages * r for at in self.labels for r in range(toks)]
            self.split = True
        labels = self.labels
        cuts = cuts or [cols]
        send = [at for at, label in enumerate(labels) if label & flag]
        keep = [at for at, label in enumerate(labels) if not label & flag]
        held = len(self.kept)
        kind = BF if self.path else F32

        def kernel(*refs):
            tok = lax.axis_index("tok")
            kept, got = refs[:held], refs[held : len(arrays)]
            keep_out, *outs = refs[len(arrays) :]

            def total(at, low, high, out_kind):
                at = (at // toks, tok ^ (at % toks)) if first else (at,)
                return add_columns(kept, got, at, low, high, out_kind)

            low = 0
            for out, width in zip(outs, cuts):
                for place, at in enumerate(send):
                    out[place] = total(at, low, low + width, BF)
                low += width
            for place, at in enumerate(keep):
                keep_out[place] = total(at, 0, cols, kind)

        stages = [
            Stage(
                kernel,
                arrays,
                [vmem()] * len(arrays),
                [like((len(keep), rows, cols), kind)]
                + [like((len(send), rows, width), BF) for width in cuts],
            )
        ]
        if rider:
            stages.append(rider.stage())
        self.count += 1
        outs = run(stages, f"{self.name}_step{self.count}", 4, after)
        self.labels = [labels[at] for at in keep]
        self.last = outs[0]
        self.kept = [outs[0]]
        self.got = [swap(piece, axis, bit) for piece in outs[1 : 1 + len(cuts)]]
        if rider:
            rider.move(outs[-1])

    def until(self, left, after=(), rider=None):
        while len(self.path) > left:
            self.halve(after, rider)

    def result(self, columns, after=()):
        kept, got = self.kept[0], self.got[0]

        def kernel(kept_ref, got_ref, *outs):
            low = 0
            for out, width in zip(outs, columns):
                cut = slice(low, low + width)
                out[...] = kept_ref[0, :, cut] + got_ref[0, :, cut].astype(F32)
                low += width

        stage = Stage(
            kernel,
            (kept, got),
            [vmem()] * 2,
            [like((kept.shape[1], width), F32) for width in columns],
        )
        return run([stage], f"{self.name}_result", 4, after)


class Direct:
    def __init__(self, terms, load, name):
        self.kept, sends = terms
        self.first = self.kept
        self.got = [swap(piece, "page", 1) for piece in sends]
        self.load, self.name = load, name

    def step(self, after):
        items, rows, cols = self.kept.shape
        toks = lax.axis_size("tok")
        sent = [like((1, rows, cols + LANES), BF)] * (items - 1)

        def kernel(kept, load, *refs):
            got, (own, load_out, *outs) = refs[: len(self.got)], refs[len(self.got) :]
            value = whole_value(two_halves(load[...]))
            value = value + whole_value(got[-1][0, :, -LANES:].astype(F32))
            load_out[...] = value
            for at in range(items):
                low = 0
                for piece in got:
                    width = min(piece.shape[2], cols - low)
                    cut = slice(low, low + width)
                    if at:
                        outs[at - 1][0, :, cut] = kept[at, :, cut] + piece[at, :, :width]
                    else:
                        own[:, cut] = kept[at, :, cut].astype(F32) + piece[at, :, :width].astype(F32)
                    low += width
            for out in outs:
                put_load(out, 0, value)

        operands = (self.kept, self.load, *self.got)
        stage = Stage(
            kernel,
            operands,
            [vmem()] * len(operands),
            [like((rows, cols), F32), like(self.load.shape, F32), *sent],
        )
        own, self.load, *sends = run([stage], f"{self.name}_step1", 6, after)
        self.last = own
        self.kept = own.reshape(toks, rows // toks, cols)
        self.got = [
            swap(piece, "page", 2 * (at + 1)).reshape(toks, rows // toks, cols + LANES)
            for at, piece in enumerate(sends)
        ]

    def along(self, after):
        toks, rows, cols = self.kept.shape
        blocks = 2 * self.load.shape[0] // rows

        def kernel(kept, load, one, two, three, own, load_out, *outs):
            tok = lax.axis_index("tok")
            halves = [
                whole_value(piece[:, :, cols:].astype(F32).reshape(toks * rows, LANES))
                for piece in (one, two, three)
            ]
            mine = whole_value(two_halves(load[...]))
            value = (mine + halves[0]) + (halves[1] + halves[2])
            load_out[...] = value
            for step in range(toks):
                at = tok ^ step
                total = kept[at] + one[at, :, :cols].astype(F32)
                total = total + two[at, :, :cols].astype(F32) + three[at, :, :cols].astype(F32)
                if step:
                    outs[step - 1][0, :, :cols] = total.astype(BF)
                    put_load(outs[step - 1], 0, value)
                else:
                    own[...] = total

        stage = Stage(
            kernel,
            (self.kept, self.load, *self.got),
            [vmem()] * 5,
            [like((rows, cols), F32), like(self.load.shape, F32)]
            + [like((1, rows, cols + blocks * LANES), BF)] * (toks - 1),
        )
        self.kept, self.load, *sends = run([stage], f"{self.name}_step2", 6, after)
        self.last = self.kept
        self.got = [swap(piece, "tok", at + 1) for at, piece in enumerate(sends)]

    def result(self, columns, after):
        rows, cols = self.kept.shape
        blocks = 2 * self.load.shape[0] // rows

        def kernel(kept, load, one, two, three, load_out, *outs):
            halves = []
            for piece in (one, two, three):
                parts = [
                    piece[0, :, cols + at * LANES :][:, :LANES].astype(F32) for at in range(blocks)
                ]
                halves.append(whole_value(jnp.concatenate(parts, 0)))
            mine = whole_value(two_halves(load[...]))
            load_out[...] = (mine + halves[0]) + (halves[1] + halves[2])
            low = 0
            for out, width in zip(outs, columns):
                cut = slice(low, low + width)
                total = kept[:, cut] + one[0, :, cut].astype(F32)
                out[...] = total + two[0, :, cut].astype(F32) + three[0, :, cut].astype(F32)
                low += width

        stage = Stage(
            kernel,
            (self.kept, self.load, *self.got),
            [vmem()] * 5,
            [like(self.load.shape, F32)] + [like((rows, width), F32) for width in columns],
        )
        load, *outs = run([stage], f"{self.name}_result", 6, after)
        self.last = load
        return outs, load


class Halved:
    def __init__(self, terms, load, name):
        self.sum = Reduction(terms, name)
        self.first = self.sum.kept[0]
        self.rider = Rider(load, list(self.sum.path))

    def step(self, after):
        self.sum.step(after, self.rider)
        self.last = self.sum.last

    def along(self, after):
        self.sum.until(0, after, self.rider)
        self.last = self.sum.last

    def result(self, columns, after):
        outs = self.sum.result(columns, after)
        self.last = outs[0]
        return outs, self.rider.pair[0] + self.rider.pair[1]


def on_device(
    tokens,
    w_query,
    w_key,
    w_value,
    w_out,
    w_inner,
    w_outer,
    gain_one,
    shift_one,
    gain_two,
    shift_two,
    table_line,
    table_horiz,
    table_vert,
    region_weight,
    region_ids,
    line_pos,
    box_horiz,
    box_vert,
    cotangent,
):
    row_count, width = tokens.shape
    shards = lax.axis_size("tok")
    rows = -(-(row_count + 2) // 16) * 16

    def padded(array_in):
        return jnp.pad(array_in, ((0, rows - row_count), (0, 0)))

    def spread(*lines):
        return jnp.concatenate(
            [jnp.pad(line, (0, 256 - row_count)) for line in lines]
            + [jnp.zeros(width - 256 * len(lines), I32)]
        )

    info = jnp.stack(
        [spread(region_ids, line_pos // 32, line_pos % 32), spread(box_horiz, box_vert)]
    ).astype(BF)
    padded_tokens = jnp.concatenate(
        [tokens, jnp.zeros((rows - row_count - 2, width), BF), info], 0
    )
    token_shards = tok_shards(padded_tokens)
    places = jnp.stack([region_ids, line_pos, box_horiz, box_vert], 1)
    query_at = jnp.pad(places, ((0, rows - row_count), (0, 4)))
    line_table = jnp.concatenate(
        [
            table_line,
            table_line + region_weight[:, None],
            jnp.full((table_line.shape[0], LANES - 2 * REL), NEG, F32),
        ],
        1,
    )
    box_table = jnp.pad(
        jnp.concatenate([table_horiz, table_vert], 1), ((0, 0), (0, LANES - 2 * REL))
    )
    vectors = jnp.stack([gain_one, shift_one, gain_two, shift_two], 0)

    w_query, w_key, w_value, w_out, w_inner, w_outer = run(
        [fetch((w_query, w_key, w_value, w_out, w_inner, w_outer))], "fetch", 1, (padded_tokens,)
    )
    first = attn_forward(
        token_shards,
        row_count,
        (w_key, w_value, w_query),
        line_table,
        box_table,
        query_at,
    )
    second = feed_forward(
        first.results[0],
        padded_tokens,
        row_count,
        w_out,
        w_inner,
        w_outer,
        vectors,
        padded(cotangent),
    )
    terms, outs = with_terms(
        [first, second],
        [[(second.results[4], second.results[7], "nn")]],
        "forward",
        10,
    )
    mix, query, keys_all, values_all, tokens_all, probs, key_at = outs[:7]
    block, hidden, n_one, r_one, active, slope, d_second, d_outer, sums_two = outs[7:]
    outer = Reduction(terms[0], "outer")
    back = feed_back(d_outer, d_second, slope, n_one, r_one, w_inner, w_outer, w_out, vectors)
    d_inner, d_first, d_attn, sums_one, d_heads = run([back], "feed_back", 8, (outer.kept[0],))
    unit = width // 6
    outer.step((d_attn,), cuts=[2 * unit, 4 * unit])
    main = 15 * unit
    terms, _ = with_terms(
        [],
        [
            [(hidden, Cut(d_inner, 0, main), "nn")],
            [(hidden, Cut(d_inner, main, w_inner.shape[1]), "nn"), (mix, d_attn, "nn")],
        ],
        "inner_terms",
        10,
        (d_attn, outer.last),
    )
    inner = Reduction(terms[0], "inner", turn=True)
    out = Reduction(terms[1], "out")
    third = width // LANES // 3

    def heads_back(at):
        return attn_back(
            d_heads, probs, query, keys_all, values_all, query_at, key_at, at * third, third
        )

    *part_one, tables_one = run([heads_back(0)], "attn_back", 10, (out.kept[0],))
    inner.step((tables_one, *outer.got[:1]), cuts=[15 * unit])
    out.step((inner.last,), cuts=[15 * unit])
    *part_two, tables_two = run(
        [heads_back(1)], "attn_more", 10, (out.last,)
    )
    stage = heads_back(2)
    parts = [part_one, part_two, stage.results[:3]]
    whole_tiles = lax.axis_size("page") == 8 and width // lax.axis_size("page") % 16 == 0
    *last_part, _, small = run(
        [stage, pack((sums_one, sums_two), (tables_one, tables_two, stage.results[3]))],
        "attn_rest",
        10,
        (tables_two,),
    )
    parts[2] = last_part

    def attn_sum(after):
        terms, _ = with_terms(
            [],
            [
                [(padded_tokens, part[0], "nn") for part in parts]
                + [(tokens_all, part[1], "nt") for part in parts]
                + [(tokens_all, part[2], "nt") for part in parts]
            ],
            "attn_terms",
            10,
            after,
            load=small if whole_tiles else None,
            cuts=[9],
        )
        return (Direct if whole_tiles else Halved)(terms[0], small, "attn")

    outer.step((small,))
    inner.step((outer.last,))
    attn = attn_sum((inner.last, ))
    d_own, rows_sent, rows_kept = run(
        [rows_back(d_first, parts, (w_query, w_key, w_value), shards)], "rows_back", 10, (attn.first,)
    )
    rows_got = swap(rows_sent, "tok", 1)
    attn.step((d_own,))
    out.step((attn.last,))
    outer.step((out.last,))
    d_own, rows_sent = run(
        [rows_step(d_own, rows_kept, rows_got)], "rows_step", 4, (outer.last,)
    )
    rows_got = swap(rows_sent, "tok", 2)
    inner.join(out)
    inner.step((d_own,))
    attn.along((inner.last,))
    outer.step((attn.last,))
    inner.step((outer.last,))
    (d_tokens,) = run([rows_result(d_own, rows_got, row_count)], "rows_result", 4, (inner.last,))
    (grad_outer,) = outer.result([width], (d_tokens,))
    grad_inner, grad_out = inner.result([w_inner.shape[1], width], (grad_outer,))
    grad_attn, small = attn.result([width] * 3, (grad_inner,))
    vector_rows = width // LANES
    vector_sums = small[: 4 * vector_rows].reshape(4, width)
    tables = small[4 * vector_rows :][: table_line.shape[0]]
    return (
        block,
        d_tokens,
        *grad_attn,
        grad_out,
        grad_inner,
        grad_outer,
        vector_sums[0],
        vector_sums[1],
        vector_sums[2],
        vector_sums[3],
        tables[:, 0:REL],
        tables[:, REL : 2 * REL],
        tables[:, 2 * REL : 3 * REL],
        tables[:, 3 * REL],
    )


def solution(mesh):
    placed = (
        P(("page", "tok"), None),
        P(),
        P(),
        P(),
        P(),
        P(),
        P(),
        P(),
        P(),
        P(),
        P(),
        P(),
        P(),
        P(),
        P(),
        P(("page", "tok")),
        P(("page", "tok")),
        P(("page", "tok")),
        P(("page", "tok")),
        P(("page", "tok"), None),
    )
    return jax.shard_map(
        on_device,
        mesh=mesh,
        in_specs=placed,
        out_specs=(
            P(("page", "tok"), None),
            P(("page", "tok"), None),
            P(("page", "tok"), None),
            P(("page", "tok"), None),
            P(("page", "tok"), None),
            P(("page", "tok"), None),
            P(("page", "tok"), None),
            P(("page", "tok"), None),
            P(),
            P(),
            P(),
            P(),
            P(),
            P(),
            P(),
            P(),
        ),
        check_vma=False,
    )
```

```python
import math

import jax
import jax.numpy as jnp
from jax import lax
from jax.experimental import pallas as pl
from jax.experimental.pallas import tpu as pltpu
from jax.sharding import PartitionSpec as P

REL = 32
BOXES = 64
BF = jnp.bfloat16
F32 = jnp.float32
I32 = jnp.int32
NEG = -1e30
LANES = 128
MIB = 2**20


def vmem():
    return pl.BlockSpec(memory_space=pltpu.VMEM)


def like(shape, kind):
    return jax.ShapeDtypeStruct(shape, kind)


class Later:
    def __init__(self, stage, index):
        self.stage, self.index = stage, index
        self.shape, self.dtype = stage.outs[index].shape, stage.outs[index].dtype


class Stage:
    def __init__(self, body, operands, specs, outs, scratch=()):
        self.body, self.operands, self.specs = body, list(operands), list(specs)
        self.outs, self.scratch = list(outs), list(scratch)
        self.results = [Later(self, index) for index in range(len(self.outs))]


def run(stages, name, limit, after=()):
    arrays, specs, place = [], [], {}
    for stage in stages:
        for operand, spec in zip(stage.operands, stage.specs):
            if not isinstance(operand, Later) and id(operand) not in place:
                place[id(operand)] = len(arrays)
                arrays.append(operand)
                specs.append(spec)
    out_shape = [out for stage in stages for out in stage.outs]

    def kernel(*refs):
        ins = refs[: len(arrays)]
        outs = list(refs[len(arrays) + len(after) :][: len(out_shape)])
        scratch = list(refs[len(arrays) + len(after) + len(out_shape) :])
        given = {}
        for stage in stages:
            own = [outs.pop(0) for _ in stage.outs]
            spare = [scratch.pop(0) for _ in stage.scratch]
            given[id(stage)] = own
            read = [
                given[id(item.stage)][item.index]
                if isinstance(item, Later)
                else ins[place[id(item)]]
                for item in stage.operands
            ]
            stage.body(*read, *own, *spare)

    return pl.pallas_call(
        kernel,
        out_shape=tuple(out_shape),
        in_specs=specs + [pl.BlockSpec(memory_space=pl.ANY)] * len(after),
        out_specs=[vmem()] * len(out_shape),
        scratch_shapes=[item for stage in stages for item in stage.scratch],
        compiler_params=pltpu.CompilerParams(vmem_limit_bytes=limit * MIB),
        name=name,
    )(*arrays, *after)


def dot_nn(left, right):
    return lax.dot_general(left, right, (((1,), (0,)), ((), ())), preferred_element_type=F32)


def dot_nt(left, right):
    return lax.dot_general(left, right, (((1,), (1,)), ((), ())), preferred_element_type=F32)


def look(table_row, index):
    return jnp.take_along_axis(jnp.broadcast_to(table_row, index.shape), index, axis=1)


def two_parts(value):
    high = value.astype(BF)
    return high, (value - high.astype(F32)).astype(BF)


def key_places(info, shard, rows, keys):
    pieces = []
    for at in range(3):
        wide = jnp.concatenate(
            [info[:, at * 256 : (at + 1) * 256], jnp.zeros((16, keys - 256), F32)], 1
        )
        pieces.append(pltpu.roll(wide, shard * rows, 1) if shard else wide)
    return pieces


def line_index(query_at, key_at):
    bucket = jnp.clip(key_at[1:2, :] - query_at[:, 1:2], -(REL // 2), REL // 2 - 1) + REL // 2
    same = jnp.where(query_at[:, 0:1] == key_at[0:1, :], REL, 0)
    return jnp.where(key_at[4:5, :] > 0, bucket + same, 2 * REL)


def attn_forward(token_shards, row_count, weights, line_table, box_table, query_at):
    rows, width = token_shards[0].shape
    head_count = line_table.shape[0]
    shards = len(token_shards)
    keys = -(-rows * shards // LANES) * LANES

    def kernel(*refs):
        tok_refs = refs[:shards]
        wk, wv, wq, line_ref, box_ref, q_at = refs[shards : shards + 6]
        mix_ref, q_ref, k_ref, v_ref, x_ref, p_ref, k_at = refs[shards + 6 : shards + 13]
        line_idx, box_idx, hots = refs[shards + 13 :]
        places = [jnp.zeros((16, keys), F32)] * 3
        for at in range(shards):
            info = tok_refs[at][rows - 16 :, :].astype(F32)
            places = [
                left + right for left, right in zip(places, key_places(info, at, rows, keys))
            ]
        lane = lax.broadcasted_iota(I32, (1, keys), 1)
        live = jnp.zeros((1, keys), I32)
        for at in range(shards):
            inside = (lane >= at * rows) & (lane < at * rows + row_count)
            live = jnp.where(inside, 1, live)
        k_at[...] = jnp.zeros_like(k_at)
        k_at[0:1] = places[0][14:15].astype(I32)
        k_at[1:2] = (places[1][14:15] * 32.0 + places[2][14:15]).astype(I32)
        k_at[2:3] = places[0][15:16].astype(I32)
        k_at[3:4] = places[1][15:16].astype(I32)
        k_at[4:5] = live
        for at in range(shards):
            x_ref[at * rows : (at + 1) * rows] = tok_refs[at][...]
        if keys > shards * rows:
            x_ref[shards * rows :] = jnp.zeros((keys - shards * rows, width), BF)
        k_ref[...] = dot_nn(x_ref[...], wk[...]).astype(BF)
        v_ref[...] = dot_nn(x_ref[...], wv[...]).astype(BF)
        q_ref[...] = (dot_nn(tok_refs[0][...], wq[...]) * 0.125).astype(BF)
        line_idx[...] = line_index(q_at, k_at)
        lane = lax.broadcasted_iota(I32, (rows, LANES), 1)
        place = jnp.where(lane < BOXES, q_at[:, 2:3], q_at[:, 3:4])
        bucket = jnp.clip((lane & (BOXES - 1)) - place, -(REL // 2), REL // 2 - 1) + REL // 2
        box_idx[...] = bucket + jnp.where(lane < BOXES, 0, REL)
        sub = lax.broadcasted_iota(I32, (LANES, keys), 0)
        place = jnp.where(sub < BOXES, k_at[2:3, :], k_at[3:4, :])
        hot = ((sub & (BOXES - 1)) == place).astype(F32).astype(BF)
        hots[0:LANES] = hot
        hots[LANES:] = hot

        def pair(at, carry):
            col = pl.ds(pl.multiple_of(at * LANES, LANES), LANES)
            q_pair, k_pair, v_pair = q_ref[:, col], k_ref[:, col], v_ref[:, col]
            mixed = []
            for half in range(2):
                head = 2 * at + half
                mine = (lane < 64) if half == 0 else (lane >= 64)
                q_one = jnp.where(mine, q_pair, jnp.zeros_like(q_pair))
                high, low = two_parts(look(box_ref[pl.ds(head, 1), :], box_idx[...]))
                score = dot_nt(q_one, k_pair) + dot_nn(jnp.concatenate([high, low], 1), hots[...])
                line_row = line_ref[pl.ds(head, 1), :]
                score = score + jnp.concatenate(
                    [
                        look(line_row, line_idx[:, cut : cut + LANES])
                        for cut in range(0, keys, LANES)
                    ],
                    1,
                )
                grown = jnp.exp(score - jnp.max(score, axis=1, keepdims=True))
                probs = grown * (1.0 / jnp.sum(grown, axis=1, keepdims=True))
                low_probs = probs.astype(BF)
                p_ref[pl.ds(head, 1)] = low_probs[None]
                mixed.append(dot_nn(low_probs, v_pair))
            mix_ref[:, col] = jnp.where(lane < 64, mixed[0], mixed[1]).astype(BF)
            return carry

        lax.fori_loop(0, width // LANES, pair, 0)

    return Stage(
        kernel,
        (*token_shards, *weights, line_table, box_table, query_at),
        [vmem()] * (shards + 6),
        (
            like((rows, width), BF),
            like((rows, width), BF),
            like((keys, width), BF),
            like((keys, width), BF),
            like((keys, width), BF),
            like((head_count, rows, keys), BF),
            like((8, keys), I32),
        ),
        [
            pltpu.VMEM((rows, keys), I32),
            pltpu.VMEM((rows, LANES), I32),
            pltpu.VMEM((2 * LANES, keys), BF),
        ],
    )


def row_mean(value):
    return jnp.mean(value, axis=1, keepdims=True)


def all_sum(value):
    return jnp.sum(jnp.sum(value, axis=1, keepdims=True), axis=0, keepdims=True)


def normal(value):
    centered = value - row_mean(value)
    scale = lax.rsqrt(row_mean(centered * centered) + 1e-05)
    return centered * scale, scale


def normal_back(d_normal, n, scale):
    return scale * (d_normal - row_mean(d_normal) - n * row_mean(d_normal * n))


FF_CUT = 512


def feed_forward(mix, tokens, row_count, w_out, w_inner, w_outer, vectors, cotangent):
    rows, width = tokens.shape

    hidden_units = w_inner.shape[1]

    def kernel(mix_ref, tok, wo, wi, wu, vec, cot, *outs):
        block, hid, n_one, r_one, act, slope, d_sec, d_out, sums, total = outs
        n, r = normal(tok[...].astype(F32) + dot_nn(mix_ref[...], wo[...]))
        n_one[...] = n
        r_one[...] = jnp.broadcast_to(r, r_one.shape)
        hidden = n * vec[0:1, :] + vec[1:2, :]
        hid[...] = hidden.astype(BF)
        total[...] = hidden
        for cut in range(0, hidden_units, FF_CUT):
            inner = dot_nn(hid[...], wi[:, cut : cut + FF_CUT])
            upper = 0.5 + 0.5 * lax.erf(inner * (0.5**0.5))
            active = (inner * upper).astype(BF)
            act[:, cut : cut + FF_CUT] = active
            bell = jnp.exp(-0.5 * inner * inner) * (2.0 * math.pi) ** -0.5
            slope[:, cut : cut + FF_CUT] = upper + inner * bell
            total[...] += dot_nn(active, wu[cut : cut + FF_CUT, :])
        n, r = normal(total[...])
        block[...] = (n * vec[2:3, :] + vec[3:4, :])[:row_count].astype(BF)
        grad = cot[...].astype(F32)
        sums[0:1, :] = jnp.sum(grad * n, axis=0, keepdims=True)
        sums[1:2, :] = jnp.sum(grad, axis=0, keepdims=True)
        second = normal_back(grad * vec[2:3, :], n, r)
        d_sec[...] = second
        d_out[...] = second.astype(BF)

    return Stage(
        kernel,
        (mix, tokens, w_out, w_inner, w_outer, vectors, cotangent),
        [vmem()] * 7,
        (
            like((row_count, width), BF),
            like((rows, width), BF),
            like((rows, width), F32),
            like((rows, LANES), F32),
            like((rows, hidden_units), BF),
            like((rows, hidden_units), F32),
            like((rows, width), F32),
            like((rows, width), BF),
            like((2, width), F32),
        ),
        [pltpu.VMEM((rows, width), F32)],
    )


def feed_back(d_outer, d_second, slope, n_one, r_one, w_inner, w_outer, w_out, vectors):
    rows, width = d_outer.shape
    hidden_units = w_inner.shape[1]

    def kernel(*refs):
        d_out, d_sec, slope_ref, n_ref, r_ref, wi, wu, wo, vec = refs[:9]
        d_in, d_first, d_attn, sums, d_heads = refs[9:]
        d_first[...] = d_sec[...]
        for cut in range(0, hidden_units, FF_CUT):
            grad = dot_nt(d_out[...], wu[cut : cut + FF_CUT, :])
            grad = (grad * slope_ref[:, cut : cut + FF_CUT]).astype(BF)
            d_in[:, cut : cut + FF_CUT] = grad
            d_first[...] += dot_nt(grad, wi[:, cut : cut + FF_CUT])
        d_hidden = d_first[...]
        n = n_ref[...]
        sums[0:1, :] = jnp.sum(d_hidden * n, axis=0, keepdims=True)
        sums[1:2, :] = jnp.sum(d_hidden, axis=0, keepdims=True)
        first = normal_back(d_hidden * vec[0:1, :], n, r_ref[:, 0:1])
        d_first[...] = first
        d_attn[...] = first.astype(BF)
        d_heads[...] = dot_nt(d_attn[...], wo[...]).astype(BF)

    return Stage(
        kernel,
        (d_outer, d_second, slope, n_one, r_one, w_inner, w_outer, w_out, vectors),
        [vmem()] * 9,
        (
            like((rows, hidden_units), BF),
            like((rows, width), F32),
            like((rows, width), BF),
            like((2, width), F32),
            like((rows, width), BF),
        ),
    )


def attn_back(
    d_heads, probs, query, keys_all, values_all, query_at, key_at, first_pair, pairs, spare=0
):
    rows, width = d_heads.shape
    columns = pairs * LANES
    head_count, _, keys = probs.shape
    half_span = REL // 2

    def kernel(*refs):
        d_ref, p_ref, q_ref, k_ref, v_ref, q_at, k_at = refs[:7]
        dkv_ref, tables = refs[7:9]
        heads_t, q_t, line_idx, key_hots, line_hots, row_hots, line_rows, rolls = refs[9:]
        base = first_pair * LANES
        heads_t[...] = d_ref[:, base : base + columns].astype(F32).T.astype(BF)
        q_t[...] = q_ref[:, base : base + columns].astype(F32).T.astype(BF)
        line_idx[...] = line_index(q_at, k_at)
        lane = lax.broadcasted_iota(I32, (rows, LANES), 1)
        sub = lax.broadcasted_iota(I32, (LANES, keys), 0)
        place = jnp.where(sub < BOXES, k_at[2:3, :], k_at[3:4, :])
        key_hots[0:LANES] = ((sub & (BOXES - 1)) == place).astype(F32).astype(BF)
        key_hots[LANES:] = (sub == k_at[0:1, :]).astype(F32).astype(BF)
        line_hots[...] = (sub == (k_at[1:2, :] & (LANES - 1))).astype(F32).astype(BF)
        place = jnp.where(lane < BOXES, q_at[:, 2:3], q_at[:, 3:4])
        row_hots[...] = ((BOXES - 1 - (lane & (BOXES - 1))) == place).astype(F32).T.astype(BF)
        line_rows[...] = (
            ((LANES - 1 - lane) == (q_at[:, 1:2] & (LANES - 1))).astype(F32).T.astype(BF)
        )
        region_hot = (lane == q_at[:, 0:1]).astype(F32)
        tables[...] = jnp.zeros_like(tables)
        rolls[...] = jnp.zeros_like(rolls)
        square_row = lax.broadcasted_iota(I32, (LANES, LANES), 0)
        square_lane = lax.broadcasted_iota(I32, (LANES, LANES), 1)
        one_lane = lax.broadcasted_iota(I32, (1, LANES), 1)
        def rolled(square):
            return jnp.sum(
                pltpu.roll(square, 0, 1, stride=1, stride_axis=0), axis=0, keepdims=True
            )

        def pair(at, carry):
            col = pl.ds(pl.multiple_of(at * LANES, LANES), LANES)
            key_col = pl.ds(pl.multiple_of(base + at * LANES, LANES), LANES)
            d_pair, k_pair, v_pair = d_ref[:, key_col], k_ref[:, key_col], v_ref[:, key_col]
            back = []
            for half in range(2):
                head = 2 * (first_pair + at) + half
                own = pl.ds(pl.multiple_of(at * LANES + 64 * half, 64), 64)
                mine = (lane < 64) if half == 0 else (lane >= 64)
                d_one = jnp.where(mine, d_pair, jnp.zeros_like(d_pair))
                d_probs = dot_nt(d_one, v_pair)
                low_probs = p_ref[head]
                p_one = low_probs.astype(F32)
                row_dot = jnp.sum(p_one * d_probs, axis=1, keepdims=True)
                d_score = p_one * (d_probs - row_dot)
                low_score = d_score.astype(BF)
                back.append(dot_nn(low_score, k_pair))
                below = pl.ds(pl.multiple_of(columns + at * LANES + 64 * half, 64), 64)
                dkv_ref[own, :] = dot_nn(q_t[own, :], low_score).astype(BF)
                dkv_ref[below, :] = dot_nn(heads_t[own, :], low_probs).astype(BF)
                at_keys = dot_nt(low_score, key_hots[...])
                in_region = all_sum(at_keys[:, LANES:] * region_hot)
                boxes = at_keys[:, :LANES]
                whole = all_sum(jnp.where(lane < BOXES, boxes, 0.0))
                high, low = two_parts(boxes)
                square = dot_nn(row_hots[...], high) + dot_nn(row_hots[...], low)
                horiz = rolled(jnp.where((square_row < 64) & (square_lane < 64), square, 0.0))
                vert = pltpu.roll(
                    jnp.where((square_row >= 64) & (square_lane >= 64), square, 0.0),
                    64,
                    1,
                    stride=1,
                    stride_axis=0,
                )
                vert = jnp.sum(vert, axis=0, keepdims=True)
                near = line_idx[...] & (REL - 1)
                wide = low_score.astype(F32)
                inside = jnp.where((near > 0) & (near < REL - 1), wide, 0.0).astype(BF)
                before = all_sum(jnp.where(near == 0, wide, 0.0))
                high, low = two_parts(dot_nt(inside, line_hots[...]))
                square = dot_nn(line_rows[...], high) + dot_nn(line_rows[...], low)
                line = rolled(square)
                within = all_sum(square)
                rolls[0, pl.ds(head, 1), :] = horiz
                rolls[1, pl.ds(head, 1), :] = vert
                rolls[2, pl.ds(head, 1), :] = line
                row = jnp.where(one_lane == 0, before, 0.0)
                row = row + jnp.where(one_lane == REL - 1, whole - before - within, 0.0)
                row = row + jnp.where(one_lane == 3 * REL, in_region, 0.0)
                tables[pl.ds(head, 1), :] = row
            dkv_ref[2 * columns : 2 * columns + rows, col] = (jnp.where(lane < 64, back[0], back[1]) * 0.125).astype(BF)
            return carry

        lax.fori_loop(0, pairs, pair, 0)
        bucket = square_lane & (REL - 1)

        def from_distance(distance):
            return jnp.clip(distance, -half_span, half_span - 1) + half_span

        horiz_map = (
            (from_distance(square_row - (BOXES - 1)) == bucket)
            & (square_lane >= REL)
            & (square_lane < 2 * REL)
        ).astype(F32)
        around = jnp.where(square_row < BOXES, square_row + 1, square_row + 1 - LANES)
        vert_map = (
            (from_distance(around) == bucket)
            & (square_lane >= 2 * REL)
            & (square_lane < 3 * REL)
        ).astype(F32)
        line_map = ((from_distance(around) == bucket) & (square_lane < REL)).astype(F32)

        def exact(left, right):
            return lax.dot_general(
                left,
                right,
                (((1,), (0,)), ((), ())),
                precision=lax.Precision.HIGHEST,
                preferred_element_type=F32,
            )

        tables[...] += (
            exact(rolls[0], horiz_map) + exact(rolls[1], vert_map) + exact(rolls[2], line_map)
        )

    return Stage(
        kernel,
        (d_heads, probs, query, keys_all, values_all, query_at, key_at),
        [vmem()] * 7,
        (
            like((2 * columns + rows + spare, keys), BF),
            like((16, LANES), F32),
        ),
        [
            pltpu.VMEM((columns, rows), BF),
            pltpu.VMEM((columns, rows), BF),
            pltpu.VMEM((rows, keys), I32),
            pltpu.VMEM((2 * LANES, keys), BF),
            pltpu.VMEM((LANES, keys), BF),
            pltpu.VMEM((LANES, rows), BF),
            pltpu.VMEM((LANES, rows), BF),
            pltpu.VMEM((3, 16, LANES), F32),
        ],
    )


def fetch(weights):
    count = len(weights)

    def kernel(*refs):
        copies = [
            pltpu.make_async_copy(far, near, refs[-1].at[at])
            for at, (far, near) in enumerate(zip(refs[:count], refs[count:-1]))
        ]
        for copy in copies:
            copy.start()
        for copy in copies:
            copy.wait()

    return Stage(
        kernel,
        weights,
        [pl.BlockSpec(memory_space=pltpu.HBM)] * count,
        [like(weight.shape, BF) for weight in weights],
        [pltpu.SemaphoreType.DMA((count,))],
    )


def rows_back(d_first, parts, weights, shards):
    rows, width = d_first.shape
    count = width // len(parts)

    def kernel(first, wq, wk, wv, *refs):
        part_refs, (own, send, keep) = refs[: len(parts)], refs[len(parts) :]
        for at in range(shards - 1, -1, -1):
            cut, total = slice(at * rows, (at + 1) * rows), None
            for group, part in enumerate(part_refs):
                col = slice(group * count, (group + 1) * count)
                value = dot_nn(wk[:, col], part[:count, cut])
                value = value + dot_nn(wv[:, col], part[count : 2 * count, cut])
                total = value if total is None else total + value
            if at % 2:
                send[at // 2] = total.T.astype(BF)
            elif at:
                keep[at // 2 - 1] = total.T.astype(BF)
            else:
                result = first[...] + total.T
                for group, part in enumerate(part_refs):
                    d_query = part[2 * count : 2 * count + rows, :count]
                    col = slice(group * count, (group + 1) * count)
                    result = result + dot_nt(d_query, wq[:, col])
                own[...] = result

    return Stage(
        kernel,
        (d_first, *weights, *parts),
        [vmem()] * (4 + len(parts)),
        (
            like((rows, width), F32),
            like((shards // 2, rows, width), BF),
            like((shards // 2 - 1, rows, width), BF),
        ),
    )


def rows_step(own, keep, got):
    def kernel(own_ref, keep_ref, got_ref, out, send):
        out[...] = own_ref[...] + got_ref[0].astype(F32)
        send[...] = keep_ref[0] + got_ref[1]

    return Stage(kernel, (own, keep, got), [vmem()] * 3, (like(own.shape, F32), like(own.shape, BF)))


def rows_result(own, got, row_count):
    def kernel(own_ref, got_ref, out):
        out[...] = (own_ref[...] + got_ref[...].astype(F32))[:row_count].astype(BF)

    return Stage(kernel, (own, got), [vmem()] * 2, (like((row_count, own.shape[1]), BF),))


def two_halves(value):
    high, low = two_parts(value)
    return jnp.concatenate([high.astype(F32), low.astype(F32)], 0)


def pack(sums, tables, spare):
    width = sums[0].shape[1]
    height = sum(item.shape[0] for item in sums) * width // LANES

    def kernel(*refs):
        out, place = refs[-1], 0
        for ref in refs[: len(sums)]:
            for row in range(ref.shape[0]):
                for cut in range(0, width, LANES):
                    out[place : place + 1] = ref[row : row + 1, cut : cut + LANES]
                    place += 1
        total = refs[len(sums)][...]
        for ref in refs[len(sums) + 1 : -2]:
            total = total + ref[...]
        out[place : place + total.shape[0]] = total
        out[place + total.shape[0] :] = jnp.zeros_like(out[place + total.shape[0] :])
        high, low = two_parts(out[...])
        below = refs[-2].shape[0] - high.shape[0]
        refs[-2][below:, :LANES] = high
        refs[-2][below:, LANES : 2 * LANES] = low

    operands = (*sums, *tables, spare)
    return Stage(
        kernel, operands, [vmem()] * len(operands), (like((-(-(height + tables[0].shape[0]) // 16) * 16, LANES), F32),)
    )


def swap(array_in, axis_name, flip):
    size = lax.axis_size(axis_name)
    return lax.ppermute(array_in, axis_name, [(at, at ^ flip) for at in range(size)])


def tok_shards(array_in):
    return [array_in] + [swap(array_in, "tok", step) for step in range(1, lax.axis_size("tok"))]


def whole_value(halves):
    return halves[: halves.shape[0] // 2] + halves[halves.shape[0] // 2 :]


def put_load(out, item, value):
    halves = two_halves(value)
    rows, cols = out.shape[1:]
    count = halves.shape[0] // rows
    for at in range(count):
        low = cols - (count - at) * LANES
        out[item, :, low : low + LANES] = halves[at * rows : (at + 1) * rows].astype(BF)


class Cut:
    def __init__(self, array, low, high):
        self.array, self.low, self.high = array, low, high


def cut_of(right, form):
    if isinstance(right, Cut):
        return right
    return Cut(right, 0, right.shape[form == "nn"])


def xor_terms(groups, cuts, load=None):
    pages = lax.axis_size("page")
    width = groups[0][0].shape[1]
    rows = width // pages
    rights = [cut_of(right, form) for _, right, form in groups]
    cols = [right.high - right.low for right in rights]
    lefts, which = [], []
    for left, _, _ in groups:
        found = [at for at, item in enumerate(lefts) if item is left]
        which.append(found[0] if found else len(lefts))
        if not found:
            lefts.append(left)

    def kernel(*refs):
        if load is not None:
            load_ref, refs = refs[0], refs[1:]
        left_refs = refs[: len(lefts)]
        right_refs = refs[len(lefts) : len(lefts) + len(groups)]
        keep, *sends = refs[len(lefts) + len(groups) :][: 1 + len(cuts)]
        rest = refs[1 + len(cuts) + len(lefts) + len(groups) :]
        turned, picked = rest[: len(lefts)], rest[len(lefts) :]
        for left_ref, turned_ref in zip(left_refs, turned):
            turned_ref[...] = (
                left_ref[...].astype(F32).T.astype(BF).reshape(pages, rows, left_ref.shape[0])
            )
        page = lax.axis_index("page")
        for odd in (1, 0):
            for at, turned_ref in enumerate(turned):
                for step in range(pages // 2):
                    picked[at][step * rows : (step + 1) * rows] = turned_ref[
                        page ^ (2 * step + odd)
                    ]
            place = 0
            outs = [out for out, count in zip(sends, cuts) for _ in range(count)]
            for at_left, right_ref, right, (_, _, form), count, out in zip(
                which, right_refs, rights, groups, cols, outs if odd else [keep] * len(groups)
            ):
                if odd and place and out is not last:
                    place = 0
                last = out
                for cut in range(0, count, 256):
                    end = min(cut + 256, count)
                    used = slice(right.low + cut, right.low + end)
                    if form == "nn":
                        value = dot_nn(picked[at_left][...], right_ref[:, used])
                    else:
                        value = dot_nt(picked[at_left][...], right_ref[used, :])
                    out[:, :, place + cut : place + end] = value.astype(BF).reshape(
                        pages // 2, rows, end - cut
                    )
                place += count
        if load is not None:
            put_load(sends[-1], 0, load_ref[...])

    sizes, first = [sum(cols)], 0
    for count in cuts:
        sizes.append(sum(cols[first : first + count]))
        first += count
    if load is not None:
        sizes[-1] += LANES
    extra = [] if load is None else [load]
    return Stage(
        kernel,
        (
            *extra,
            *lefts,
            *[right.array for right in rights],
        ),
        [vmem()] * (len(extra) + len(lefts) + len(groups)),
        [like((pages // 2, rows, size), BF) for size in sizes],
        [pltpu.VMEM((pages, rows, left.shape[0]), BF) for left in lefts]
        + [pltpu.VMEM((pages // 2 * rows, left.shape[0]), BF) for left in lefts],
    )


def plain_terms(groups):
    pages, parts = lax.axis_size("page"), []
    for left, right, form in groups:
        cut = cut_of(right, form)
        side = int(form == "nn")
        used = lax.slice_in_dim(cut.array, cut.low, cut.high, axis=side)
        part = lax.dot_general(
            left, used, (((0,), (1 - side,)), ((), ())), preferred_element_type=F32
        )
        parts.append(part.astype(BF))
    whole = jnp.concatenate(parts, 1)
    whole = whole.reshape(pages, whole.shape[0] // pages, whole.shape[1])
    whole = jnp.take(whole, lax.axis_index("page") ^ jnp.arange(pages), axis=0)
    return whole[0::2], [whole[1::2]]


def with_terms(stages, sums, name, limit, after=(), load=None, cuts=None):
    width, pages = sums[0][0][0].shape[1], lax.axis_size("page")
    if width // pages % 16:
        outs = run(stages, name, limit, after) if stages else ()
        order = [item for stage in stages for item in stage.results]

        def real(item):
            return outs[order.index(item)] if isinstance(item, Later) else item

        return [
            plain_terms([(real(left), real(right), form) for left, right, form in groups])
            for groups in sums
        ], outs
    last = [xor_terms(groups, cuts or [len(groups)], load) for groups in sums]
    outs = run([*stages, *last], name, limit, after)
    each = 1 + len(cuts or [0])
    count = len(outs) - each * len(sums)
    terms = [(outs[at], list(outs[at + 1 : at + each])) for at in range(count, len(outs), each)]
    return terms, outs[:count]


def plain_sum(pair):
    def kernel(left, right, out):
        out[...] = left[...] + right[...]

    return Stage(kernel, pair, [vmem()] * 2, (like(pair[0].shape, pair[0].dtype),))


class Rider:
    def __init__(self, vector, path):
        self.path = [("page", 1)] + path
        self.move(vector)

    def stage(self):
        return plain_sum(self.pair)

    def move(self, vector):
        self.pair = (vector, swap(vector, *self.path.pop(0)))


def add_columns(kept, got, at, low, high, kind):
    ends = set()
    for pieces in (kept, got):
        place = 0
        for piece in pieces:
            place += piece.shape[-1]
            ends.add(place)
    ends = sorted(end for end in ends if low < end < high) + [high]

    def read(pieces, first, last):
        place = 0
        for piece in pieces:
            if place <= first and last <= place + piece.shape[-1]:
                return piece[(*at, slice(None), slice(first - place, last - place))].astype(kind)
            place += piece.shape[-1]

    values, first = [], low
    for end in ends:
        values.append(read(kept, first, end) + read(got, first, end))
        first = end
    return values[0] if len(values) == 1 else jnp.concatenate(values, 1)


class Reduction:
    def __init__(self, terms, name, turn=False, tok_first=False):
        keep, sends = terms
        pages, toks = lax.axis_size("page"), lax.axis_size("tok")
        self.name, self.count, self.pages, self.toks = name, 0, pages, toks
        bits = [1 << at for at in range(1, pages.bit_length() - 1)]
        page_path = [("page", bit) for bit in (bits[::-1] if turn else bits)]
        tok_path = [("tok", 1 << at) for at in range(toks.bit_length() - 1)]
        self.path = tok_path + page_path if tok_first else page_path + tok_path
        self.labels, self.split = list(range(0, pages, 2)), False
        self.kept, self.got = [keep], [swap(piece, "page", 1) for piece in sends]

    def join(self, other):
        self.kept, self.got = self.kept + other.kept, self.got + other.got

    def step(self, after=(), rider=None, cuts=None):
        begun = self.count > 0
        self.halve(after, rider, cuts)
        while begun and self.path and self.path[0][0] == "page":
            self.halve(after, rider)

    def halve(self, after=(), rider=None, cuts=None):
        axis, bit = self.path.pop(0)
        flag = bit if axis == "page" else bit * self.pages
        first = axis == "tok" and not self.split
        arrays, toks = [*self.kept, *self.got], self.toks
        rows, cols = self.kept[0].shape[1], sum(array.shape[2] for array in self.kept)
        if first:
            rows //= toks
            arrays = [a.reshape(a.shape[0], toks, rows, a.shape[2]) for a in arrays]
            self.labels = [at + self.pages * r for at in self.labels for r in range(toks)]
            self.split = True
        labels = self.labels
        cuts = cuts or [cols]
        send = [at for at, label in enumerate(labels) if label & flag]
        keep = [at for at, label in enumerate(labels) if not label & flag]
        held = len(self.kept)
        kind = BF if self.path else F32

        def kernel(*refs):
            tok = lax.axis_index("tok")
            kept, got = refs[:held], refs[held : len(arrays)]
            keep_out, *outs = refs[len(arrays) :]

            def total(at, low, high, out_kind):
                at = (at // toks, tok ^ (at % toks)) if first else (at,)
                return add_columns(kept, got, at, low, high, out_kind)

            low = 0
            for out, width in zip(outs, cuts):
                for place, at in enumerate(send):
                    out[place] = total(at, low, low + width, BF)
                low += width
            for place, at in enumerate(keep):
                keep_out[place] = total(at, 0, cols, kind)

        stages = [
            Stage(
                kernel,
                arrays,
                [vmem()] * len(arrays),
                [like((len(keep), rows, cols), kind)]
                + [like((len(send), rows, width), BF) for width in cuts],
            )
        ]
        if rider:
            stages.append(rider.stage())
        self.count += 1
        outs = run(stages, f"{self.name}_step{self.count}", 4, after)
        self.labels = [labels[at] for at in keep]
        self.last = outs[0]
        self.kept = [outs[0]]
        self.got = [swap(piece, axis, bit) for piece in outs[1 : 1 + len(cuts)]]
        if rider:
            rider.move(outs[-1])

    def until(self, left, after=(), rider=None):
        while len(self.path) > left:
            self.halve(after, rider)

    def result(self, columns, after=(), side=None):
        held, rows = len(self.kept), self.kept[0].shape[1]
        sides = [] if side is None else [side]
        extra = 0 if side is None else side.shape[1]

        def kernel(*refs):
            ins, outs = refs[: -len(columns)], refs[-len(columns) :]
            kept, got, low = ins[:held], ins[held : held + len(self.got)], 0
            for out, width in zip(outs, columns):
                own = width - (extra if out is outs[-1] else 0)
                out[:, :own] = add_columns(kept, got, (0,), low, low + own, F32)
                low += own
            if sides:
                outs[-1][:, columns[-1] - extra :] = ins[-1][...]

        stage = Stage(
            kernel,
            (*self.kept, *self.got, *sides),
            [vmem()] * (held + len(self.got) + len(sides)),
            [like((rows, width), F32) for width in columns],
        )
        return run([stage], f"{self.name}_result", 4, after)


class Direct:
    def __init__(self, tokens_pair, parts_pair, load, side, rows, name, after):
        pages, toks = lax.axis_size("page"), lax.axis_size("tok")
        items, keys = pages // 2, tokens_pair[0].shape[0]
        share = tokens_pair[0].shape[1] // pages
        cols = 3 * tokens_pair[0].shape[1]
        count = cols // 3 // len(parts_pair)
        extra = side.kept[0].shape[2]
        self.name = name

        def kernel(mine, other, load_ref, side_kept, side_got, *refs):
            part_refs, refs = refs[: 2 * len(parts_pair)], refs[2 * len(parts_pair) :]
            own, load_out, side_own = refs[:3]
            outs, (turned, picked) = refs[3 : 2 + items], refs[2 + items :]
            page = lax.axis_index("page")
            for which, ref in enumerate((mine, other)):
                turned[...] = ref[...].astype(F32).T.astype(BF).reshape(pages, share, keys)
                for at in range(items):
                    picked[which, at * share : (at + 1) * share] = turned[page ^ (2 * at)]
            for group in range(len(parts_pair)):
                for kind in range(3):
                    total = None
                    for which in range(2):
                        part = part_refs[2 * group + which]
                        if kind == 0:
                            d_query = part[2 * count : 2 * count + rows, :count]
                            value = dot_nn(picked[which, :, :rows], d_query)
                        else:
                            used = slice((kind - 1) * count, kind * count)
                            value = dot_nt(picked[which], part[used, :])
                        total = value if total is None else total + value
                    place = kind * (cols // 3) + group * count
                    col = slice(place, place + count)
                    own[:, col] = total[:share]
                    for at in range(1, items):
                        outs[at - 1][0, :, col] = total[at * share : (at + 1) * share].astype(BF)
            below = part_refs[-1]
            height = load_ref.shape[0]
            value = below[-height:, :LANES].astype(F32) + below[-height:, LANES : 2 * LANES].astype(
                F32
            )
            value = whole_value(two_halves(load_ref[...])) + value
            load_out[...] = value
            side_own[...] = side_kept[0].astype(F32) + side_got[0].astype(F32)
            for at in range(1, items):
                outs[at - 1][0, :, cols : cols + extra] = side_kept[at] + side_got[at]
                put_load(outs[at - 1], 0, value)

        flat = [part for pair in parts_pair for part in pair]
        operands = (*tokens_pair, load, side.kept[0], side.got[0], *flat)
        stage = Stage(
            kernel,
            operands,
            [vmem()] * len(operands),
            [
                like((share, cols), F32),
                like(load.shape, F32),
                like((share, extra), F32),
                *[like((1, share, cols + extra + LANES), BF)] * (items - 1),
            ],
            [
                pltpu.VMEM((pages, share, keys), BF),
                pltpu.VMEM((2, items * share, keys), BF),
            ],
        )
        own, self.load, self.side_own, *sends = run([stage], f"{name}_terms", 10, after)
        self.first = own
        self.kept = own.reshape(toks, share // toks, cols)
        self.got = [
            swap(piece, "page", 2 * (at + 1)).reshape(toks, share // toks, cols + extra + LANES)
            for at, piece in enumerate(sends)
        ]

    def along(self, after):
        toks, rows, cols = self.kept.shape
        blocks = 2 * self.load.shape[0] // rows
        extra = self.side_own.shape[1]

        def kernel(kept, load, side_own, one, two, three, own, load_out, side_out, *outs):
            tok = lax.axis_index("tok")
            for at in range(toks):
                total = side_own[at * rows : (at + 1) * rows]
                for piece in (one, two, three):
                    total = total + piece[at, :, cols : cols + extra].astype(F32)
                side_out[at * rows : (at + 1) * rows] = total
            halves = [
                whole_value(piece[:, :, cols + extra :].astype(F32).reshape(toks * rows, LANES))
                for piece in (one, two, three)
            ]
            mine = whole_value(two_halves(load[...]))
            value = (mine + halves[0]) + (halves[1] + halves[2])
            load_out[...] = value
            for step in range(toks):
                at = tok ^ step
                total = kept[at] + one[at, :, :cols].astype(F32)
                total = total + two[at, :, :cols].astype(F32) + three[at, :, :cols].astype(F32)
                if step:
                    outs[step - 1][0, :, :cols] = total.astype(BF)
                    put_load(outs[step - 1], 0, value)
                else:
                    own[...] = total

        stage = Stage(
            kernel,
            (self.kept, self.load, self.side_own, *self.got),
            [vmem()] * 6,
            [
                like((rows, cols), F32),
                like(self.load.shape, F32),
                like((toks * rows, extra), F32),
            ]
            + [like((1, rows, cols + blocks * LANES), BF)] * (toks - 1),
        )
        self.kept, self.load, self.side_sum, *sends = run(
            [stage], f"{self.name}_step2", 6, after
        )
        self.last = self.kept
        self.got = [swap(piece, "tok", at + 1) for at, piece in enumerate(sends)]

    def result(self, columns, after):
        rows, cols = self.kept.shape
        blocks = 2 * self.load.shape[0] // rows

        def kernel(kept, load, one, two, three, load_out, *outs):
            halves = []
            for piece in (one, two, three):
                parts = [
                    piece[0, :, cols + at * LANES :][:, :LANES].astype(F32) for at in range(blocks)
                ]
                halves.append(whole_value(jnp.concatenate(parts, 0)))
            mine = whole_value(two_halves(load[...]))
            load_out[...] = (mine + halves[0]) + (halves[1] + halves[2])
            low = 0
            for out, width in zip(outs, columns):
                cut = slice(low, low + width)
                total = kept[:, cut] + one[0, :, cut].astype(F32)
                out[...] = total + two[0, :, cut].astype(F32) + three[0, :, cut].astype(F32)
                low += width

        stage = Stage(
            kernel,
            (self.kept, self.load, *self.got),
            [vmem()] * 5,
            [like(self.load.shape, F32)] + [like((rows, width), F32) for width in columns],
        )
        load, *outs = run([stage], f"{self.name}_result", 6, after)
        self.last = load
        return outs, load


class Halved:
    def __init__(self, terms, load, name, side):
        self.sum, self.side = Reduction(terms, name), side
        self.first = self.sum.kept[0]
        self.rider = Rider(load, list(self.sum.path))

    def along(self, after):
        self.sum.until(0, after, self.rider)
        self.side.until(0, (self.sum.last,))
        self.last = self.side.last
        self.side_sum = self.side.kept[0][0] + self.side.got[0][0].astype(F32)

    def result(self, columns, after):
        outs = self.sum.result(columns, after)
        self.last = outs[0]
        return outs, self.rider.pair[0] + self.rider.pair[1]


def on_device(
    tokens,
    w_query,
    w_key,
    w_value,
    w_out,
    w_inner,
    w_outer,
    gain_one,
    shift_one,
    gain_two,
    shift_two,
    table_line,
    table_horiz,
    table_vert,
    region_weight,
    region_ids,
    line_pos,
    box_horiz,
    box_vert,
    cotangent,
):
    row_count, width = tokens.shape
    shards = lax.axis_size("tok")
    rows = -(-(row_count + 2) // 16) * 16

    def padded(array_in):
        return jnp.pad(array_in, ((0, rows - row_count), (0, 0)))

    def spread(*lines):
        return jnp.concatenate(
            [jnp.pad(line, (0, 256 - row_count)) for line in lines]
            + [jnp.zeros(width - 256 * len(lines), I32)]
        )

    info = jnp.stack(
        [spread(region_ids, line_pos // 32, line_pos % 32), spread(box_horiz, box_vert)]
    ).astype(BF)
    padded_tokens = jnp.concatenate(
        [tokens, jnp.zeros((rows - row_count - 2, width), BF), info], 0
    )
    token_shards = tok_shards(padded_tokens)
    places = jnp.stack([region_ids, line_pos, box_horiz, box_vert], 1)
    query_at = jnp.pad(places, ((0, rows - row_count), (0, 4)))
    line_table = jnp.concatenate(
        [
            table_line,
            table_line + region_weight[:, None],
            jnp.full((table_line.shape[0], LANES - 2 * REL), NEG, F32),
        ],
        1,
    )
    box_table = jnp.pad(
        jnp.concatenate([table_horiz, table_vert], 1), ((0, 0), (0, LANES - 2 * REL))
    )
    vectors = jnp.stack([gain_one, shift_one, gain_two, shift_two], 0)

    w_query, w_key, w_value, w_out, w_inner, w_outer = run(
        [fetch((w_query, w_key, w_value, w_out, w_inner, w_outer))], "fetch", 1, (padded_tokens,)
    )
    first = attn_forward(
        token_shards,
        row_count,
        (w_key, w_value, w_query),
        line_table,
        box_table,
        query_at,
    )
    second = feed_forward(
        first.results[0],
        padded_tokens,
        row_count,
        w_out,
        w_inner,
        w_outer,
        vectors,
        padded(cotangent),
    )
    unit = width // 6
    terms, outs = with_terms(
        [first, second],
        [
            [(second.results[4], Cut(second.results[7], 0, 4 * unit), "nn")],
            [(second.results[4], Cut(second.results[7], 4 * unit, width), "nn")],
        ],
        "forward",
        10,
    )
    mix, query, keys_all, values_all, tokens_all, probs, key_at = outs[:7]
    block, hidden, n_one, r_one, active, slope, d_second, d_outer, sums_two = outs[7:]
    outer = Reduction(terms[0], "outer")
    zed = Reduction(terms[1], "zed", tok_first=True)
    back = feed_back(d_outer, d_second, slope, n_one, r_one, w_inner, w_outer, w_out, vectors)
    d_inner, d_first, d_attn, sums_one, d_heads = run([back], "feed_back", 8, (outer.kept[0],))
    outer.step((d_attn,), cuts=[2 * unit, 2 * unit])
    zed.halve((outer.last,))
    main = 16 * unit
    terms, _ = with_terms(
        [],
        [
            [(hidden, Cut(d_inner, 0, main), "nn")],
            [(hidden, Cut(d_inner, main, w_inner.shape[1]), "nn"), (mix, d_attn, "nn")],
        ],
        "inner_terms",
        10,
        (d_attn, zed.last),
    )
    inner = Reduction(terms[0], "inner", turn=True)
    out = Reduction(terms[1], "out")
    whole_tiles = lax.axis_size("page") == 8 and width // lax.axis_size("page") % 16 == 0
    third = width // LANES // 3

    def heads_back(at, spare=0):
        return attn_back(
            d_heads, probs, query, keys_all, values_all, query_at, key_at, at * third, third, spare
        )

    def beside(array):
        return [swap(array, "page", 1)] if whole_tiles else []

    other_tokens = beside(tokens_all)

    part_one, tables_one = run([heads_back(0)], "attn_back", 10, (out.kept[0], ))
    zed.halve((tables_one, *outer.got[:1]))
    inner.step((zed.last,), cuts=[16 * unit])
    out.step((inner.last,), cuts=[14 * unit])
    others = beside(part_one)
    part_two, tables_two = run(
        [heads_back(1)], "attn_more", 10, (out.last,)
    )
    others += beside(part_two)
    stage = heads_back(2, 48)
    last_part, _, small = run(
        [stage, pack((sums_one, sums_two), (tables_one, tables_two, stage.results[1]), stage.results[0])],
        "attn_rest",
        10,
        (tables_two,),
    )
    parts = [part_one, part_two, last_part]
    others += beside(last_part)

    def attn_sum(after):
        if whole_tiles:
            return Direct(
                (tokens_all, *other_tokens),
                list(zip(parts, others)),
                small,
                zed,
                rows,
                "attn",
                after,
            )
        count = width // len(parts)
        groups = (
            [(padded_tokens, part[2 * count :][:rows, :count], "nn") for part in parts]
            + [(tokens_all, Cut(part, 0, count), "nt") for part in parts]
            + [(tokens_all, Cut(part, count, 2 * count), "nt") for part in parts]
        )
        return Halved(plain_terms(groups), small, "attn", zed)

    outer.step((small,))
    inner.step((outer.last, *others[0:1]))
    d_own, rows_sent, rows_kept = run(
        [rows_back(d_first, parts, (w_query, w_key, w_value), shards)], "rows_back", 10, (inner.last,)
    )
    rows_got = swap(rows_sent, "tok", 1)
    out.step((d_own, *others[1:2]))
    attn = attn_sum((out.last, *outer.got[:3], *inner.got[:2]))
    d_own, rows_sent = run(
        [rows_step(d_own, rows_kept, rows_got)], "rows_step", 4, (attn.first,)
    )
    rows_got = swap(rows_sent, "tok", 2)
    inner.join(out)
    inner.step((d_own,))
    outer.step((inner.last,))
    (d_tokens,) = run([rows_result(d_own, rows_got, row_count)], "rows_result", 4, (outer.last,))
    inner.step((d_tokens,))
    outer.step((inner.last,))
    attn.along((outer.last,))
    grad_inner, grad_out = inner.result([w_inner.shape[1], width], (attn.last,))
    (grad_outer,) = outer.result([width], (grad_inner,), attn.side_sum)
    grad_attn, small = attn.result([width] * 3, (grad_outer,))
    vector_rows = width // LANES
    vector_sums = small[: 4 * vector_rows].reshape(4, width)
    tables = small[4 * vector_rows :][: table_line.shape[0]]
    return (
        block,
        d_tokens,
        *grad_attn,
        grad_out,
        grad_inner,
        grad_outer,
        vector_sums[0],
        vector_sums[1],
        vector_sums[2],
        vector_sums[3],
        tables[:, 0:REL],
        tables[:, REL : 2 * REL],
        tables[:, 2 * REL : 3 * REL],
        tables[:, 3 * REL],
    )


def solution(mesh):
    placed = (
        P(("page", "tok"), None),
        P(),
        P(),
        P(),
        P(),
        P(),
        P(),
        P(),
        P(),
        P(),
        P(),
        P(),
        P(),
        P(),
        P(),
        P(("page", "tok")),
        P(("page", "tok")),
        P(("page", "tok")),
        P(("page", "tok")),
        P(("page", "tok"), None),
    )
    return jax.shard_map(
        on_device,
        mesh=mesh,
        in_specs=placed,
        out_specs=(
            P(("page", "tok"), None),
            P(("page", "tok"), None),
            P(("page", "tok"), None),
            P(("page", "tok"), None),
            P(("page", "tok"), None),
            P(("page", "tok"), None),
            P(("page", "tok"), None),
            P(("page", "tok"), None),
            P(),
            P(),
            P(),
            P(),
            P(),
            P(),
            P(),
            P(),
        ),
        check_vma=False,
    )
```

```python
import math

import jax
import jax.numpy as jnp
from jax import lax
from jax.experimental import pallas as pl
from jax.experimental.pallas import tpu as pltpu
from jax.sharding import PartitionSpec as P

REL = 32
BOXES = 64
BF = jnp.bfloat16
F32 = jnp.float32
I32 = jnp.int32
NEG = -1e30
LANES = 128
MIB = 2**20


def vmem():
    return pl.BlockSpec(memory_space=pltpu.VMEM)


def like(shape, kind):
    return jax.ShapeDtypeStruct(shape, kind)


class Later:
    def __init__(self, stage, index):
        self.stage, self.index = stage, index
        self.shape, self.dtype = stage.outs[index].shape, stage.outs[index].dtype


class Stage:
    def __init__(self, body, operands, specs, outs, scratch=()):
        self.body, self.operands, self.specs = body, list(operands), list(specs)
        self.outs, self.scratch = list(outs), list(scratch)
        self.results = [Later(self, index) for index in range(len(self.outs))]


def run(stages, name, limit, after=()):
    arrays, specs, place = [], [], {}
    for stage in stages:
        for operand, spec in zip(stage.operands, stage.specs):
            if not isinstance(operand, Later) and id(operand) not in place:
                place[id(operand)] = len(arrays)
                arrays.append(operand)
                specs.append(spec)
    out_shape = [out for stage in stages for out in stage.outs]

    def kernel(*refs):
        ins = refs[: len(arrays)]
        outs = list(refs[len(arrays) + len(after) :][: len(out_shape)])
        scratch = list(refs[len(arrays) + len(after) + len(out_shape) :])
        given = {}
        for stage in stages:
            own = [outs.pop(0) for _ in stage.outs]
            spare = [scratch.pop(0) for _ in stage.scratch]
            given[id(stage)] = own
            read = [
                given[id(item.stage)][item.index]
                if isinstance(item, Later)
                else ins[place[id(item)]]
                for item in stage.operands
            ]
            stage.body(*read, *own, *spare)

    return pl.pallas_call(
        kernel,
        out_shape=tuple(out_shape),
        in_specs=specs + [pl.BlockSpec(memory_space=pl.ANY)] * len(after),
        out_specs=[vmem()] * len(out_shape),
        scratch_shapes=[item for stage in stages for item in stage.scratch],
        compiler_params=pltpu.CompilerParams(vmem_limit_bytes=limit * MIB),
        name=name,
    )(*arrays, *after)


def dot_nn(left, right):
    return lax.dot_general(left, right, (((1,), (0,)), ((), ())), preferred_element_type=F32)


def dot_nt(left, right):
    return lax.dot_general(left, right, (((1,), (1,)), ((), ())), preferred_element_type=F32)


def look(table_row, index):
    return jnp.take_along_axis(jnp.broadcast_to(table_row, index.shape), index, axis=1)


def two_parts(value):
    high = value.astype(BF)
    return high, (value - high.astype(F32)).astype(BF)


def key_places(info, shard, rows, keys):
    pieces = []
    for at in range(3):
        wide = jnp.concatenate(
            [info[:, at * 256 : (at + 1) * 256], jnp.zeros((16, keys - 256), F32)], 1
        )
        pieces.append(pltpu.roll(wide, shard * rows, 1) if shard else wide)
    return pieces


def line_index(query_at, key_at):
    bucket = jnp.clip(key_at[1:2, :] - query_at[:, 1:2], -(REL // 2), REL // 2 - 1) + REL // 2
    same = jnp.where(query_at[:, 0:1] == key_at[0:1, :], REL, 0)
    return jnp.where(key_at[4:5, :] > 0, bucket + same, 2 * REL)


def with_places(tokens, places, rows):
    count, width = tokens.shape

    def kernel(tok, region, line, horiz, vert, out, work):
        work[:count] = tok[...].astype(F32)
        work[count:] = jnp.zeros((rows - count, width), F32)
        lines = (
            (rows - 2, 0, region[...]),
            (rows - 2, 256, line[...] >> 5),
            (rows - 2, 512, line[...] & 31),
            (rows - 1, 0, horiz[...]),
            (rows - 1, 256, vert[...]),
        )
        for row, lane, value in lines:
            work[row : row + 1, lane : lane + count] = value.astype(F32).reshape(1, count)
        out[...] = work[...].astype(BF)

    return Stage(
        kernel,
        (tokens, *places),
        [vmem()] * 5,
        (like((rows, width), BF),),
        [pltpu.VMEM((rows, width), F32)],
    )


def first_rows(token_shards, weights):
    rows, width = token_shards[0].shape
    shards = len(token_shards)

    def kernel(*refs):
        tok_refs, (wk, wv, wq, q_ref, k_ref, v_ref, x_ref) = refs[:shards], refs[shards:]
        for at in range(shards):
            x_ref[at * rows : (at + 1) * rows] = tok_refs[at][...]
        q_ref[...] = (dot_nn(tok_refs[0][...], wq[...]) * 0.125).astype(BF)
        k_ref[...] = dot_nn(x_ref[...], wk[...]).astype(BF)
        v_ref[...] = dot_nn(x_ref[...], wv[...]).astype(BF)

    return Stage(
        kernel,
        (*token_shards, *weights),
        [vmem()] * (shards + 3),
        (
            like((rows, width), BF),
            like((shards * rows, width), BF),
            like((shards * rows, width), BF),
        ),
        [pltpu.VMEM((shards * rows, width), BF)],
    )


def attn_forward(token_shards, row_count, ready, weights, line_table, box_table, query_at):
    rows, width = token_shards[0].shape
    head_count = line_table.shape[0]
    shards = len(token_shards)
    keys = -(-rows * shards // LANES) * LANES

    def kernel(*refs):
        tok_refs = refs[:shards]
        q_in, k_in, v_in, wk, wv, line_ref, box_ref, q_at = refs[shards : shards + 8]
        mix_ref, q_ref, k_ref, v_ref, x_ref, p_ref, k_at = refs[shards + 8 : shards + 15]
        line_idx, box_idx, hots = refs[shards + 15 :]
        places = [jnp.zeros((16, keys), F32)] * 3
        for at in range(shards):
            info = tok_refs[at][rows - 16 :, :].astype(F32)
            places = [
                left + right for left, right in zip(places, key_places(info, at, rows, keys))
            ]
        lane = lax.broadcasted_iota(I32, (1, keys), 1)
        live = jnp.zeros((1, keys), I32)
        for at in range(shards):
            inside = (lane >= at * rows) & (lane < at * rows + row_count)
            live = jnp.where(inside, 1, live)
        k_at[...] = jnp.zeros_like(k_at)
        k_at[0:1] = places[0][14:15].astype(I32)
        k_at[1:2] = (places[1][14:15] * 32.0 + places[2][14:15]).astype(I32)
        k_at[2:3] = places[0][15:16].astype(I32)
        k_at[3:4] = places[1][15:16].astype(I32)
        k_at[4:5] = live
        for at in range(shards):
            x_ref[at * rows : (at + 1) * rows] = tok_refs[at][...]
        if keys > shards * rows:
            x_ref[shards * rows :] = jnp.zeros((keys - shards * rows, width), BF)
        done = k_in.shape[0]
        q_ref[...] = q_in[...]
        k_ref[:done] = k_in[...]
        v_ref[:done] = v_in[...]
        k_ref[done:] = dot_nn(x_ref[done:], wk[...]).astype(BF)
        v_ref[done:] = dot_nn(x_ref[done:], wv[...]).astype(BF)
        line_idx[...] = line_index(q_at, k_at)
        lane = lax.broadcasted_iota(I32, (rows, LANES), 1)
        place = jnp.where(lane < BOXES, q_at[:, 2:3], q_at[:, 3:4])
        bucket = jnp.clip((lane & (BOXES - 1)) - place, -(REL // 2), REL // 2 - 1) + REL // 2
        box_idx[...] = bucket + jnp.where(lane < BOXES, 0, REL)
        sub = lax.broadcasted_iota(I32, (LANES, keys), 0)
        place = jnp.where(sub < BOXES, k_at[2:3, :], k_at[3:4, :])
        hot = ((sub & (BOXES - 1)) == place).astype(F32).astype(BF)
        hots[0:LANES] = hot
        hots[LANES:] = hot

        def pair(at, carry):
            col = pl.ds(pl.multiple_of(at * LANES, LANES), LANES)
            q_pair, k_pair, v_pair = q_ref[:, col], k_ref[:, col], v_ref[:, col]
            mixed = []
            for half in range(2):
                head = 2 * at + half
                mine = (lane < 64) if half == 0 else (lane >= 64)
                q_one = jnp.where(mine, q_pair, jnp.zeros_like(q_pair))
                high, low = two_parts(look(box_ref[pl.ds(head, 1), :], box_idx[...]))
                score = dot_nt(q_one, k_pair) + dot_nn(jnp.concatenate([high, low], 1), hots[...])
                line_row = line_ref[pl.ds(head, 1), :]
                score = score + jnp.concatenate(
                    [
                        look(line_row, line_idx[:, cut : cut + LANES])
                        for cut in range(0, keys, LANES)
                    ],
                    1,
                )
                grown = jnp.exp(score - jnp.max(score, axis=1, keepdims=True))
                probs = grown * (1.0 / jnp.sum(grown, axis=1, keepdims=True))
                low_probs = probs.astype(BF)
                p_ref[pl.ds(head, 1)] = low_probs[None]
                mixed.append(dot_nn(low_probs, v_pair))
            mix_ref[:, col] = jnp.where(lane < 64, mixed[0], mixed[1]).astype(BF)
            return carry

        lax.fori_loop(0, width // LANES, pair, 0)

    return Stage(
        kernel,
        (*token_shards, *ready, *weights, line_table, box_table, query_at),
        [vmem()] * (shards + 8),
        (
            like((rows, width), BF),
            like((rows, width), BF),
            like((keys, width), BF),
            like((keys, width), BF),
            like((keys, width), BF),
            like((head_count, rows, keys), BF),
            like((8, keys), I32),
        ),
        [
            pltpu.VMEM((rows, keys), I32),
            pltpu.VMEM((rows, LANES), I32),
            pltpu.VMEM((2 * LANES, keys), BF),
        ],
    )


def row_mean(value):
    return jnp.mean(value, axis=1, keepdims=True)


def all_sum(value):
    return jnp.sum(jnp.sum(value, axis=1, keepdims=True), axis=0, keepdims=True)


def normal(value):
    centered = value - row_mean(value)
    scale = lax.rsqrt(row_mean(centered * centered) + 1e-05)
    return centered * scale, scale


def normal_back(d_normal, n, scale):
    return scale * (d_normal - row_mean(d_normal) - n * row_mean(d_normal * n))


FF_CUT = 512


def feed_forward(mix, tokens, row_count, w_out, w_inner, w_outer, vectors, cotangent):
    rows, width = tokens.shape

    hidden_units = w_inner.shape[1]

    def kernel(mix_ref, tok, wo, wi, wu, cot, *refs):
        vec = [ref[...].reshape(1, width) for ref in refs[:4]]
        block, hid, n_one, r_one, act, slope, d_sec, d_out, sums, total = refs[4:]
        n, r = normal(tok[...].astype(F32) + dot_nn(mix_ref[...], wo[...]))
        n_one[...] = n
        r_one[...] = jnp.broadcast_to(r, r_one.shape)
        hidden = n * vec[0] + vec[1]
        hid[...] = hidden.astype(BF)
        total[...] = hidden
        for cut in range(0, hidden_units, FF_CUT):
            inner = dot_nn(hid[...], wi[:, cut : cut + FF_CUT])
            upper = 0.5 + 0.5 * lax.erf(inner * (0.5**0.5))
            active = (inner * upper).astype(BF)
            act[:, cut : cut + FF_CUT] = active
            bell = jnp.exp(-0.5 * inner * inner) * (2.0 * math.pi) ** -0.5
            slope[:, cut : cut + FF_CUT] = upper + inner * bell
            total[...] += dot_nn(active, wu[cut : cut + FF_CUT, :])
        n, r = normal(total[...])
        block[...] = (n * vec[2] + vec[3])[:row_count].astype(BF)
        total[:row_count] = cot[...].astype(F32)
        total[row_count:] = jnp.zeros((rows - row_count, width), F32)
        grad = total[...]
        sums[0:1, :] = jnp.sum(grad * n, axis=0, keepdims=True)
        sums[1:2, :] = jnp.sum(grad, axis=0, keepdims=True)
        second = normal_back(grad * vec[2], n, r)
        d_sec[...] = second
        d_out[...] = second.astype(BF)

    return Stage(
        kernel,
        (mix, tokens, w_out, w_inner, w_outer, cotangent, *vectors),
        [vmem()] * 10,
        (
            like((row_count, width), BF),
            like((rows, width), BF),
            like((rows, width), F32),
            like((rows, LANES), F32),
            like((rows, hidden_units), BF),
            like((rows, hidden_units), F32),
            like((rows, width), F32),
            like((rows, width), BF),
            like((2, width), F32),
        ),
        [pltpu.VMEM((rows, width), F32)],
    )


def feed_back(d_outer, d_second, slope, n_one, r_one, w_inner, w_outer, w_out, gain_one):
    rows, width = d_outer.shape
    hidden_units = w_inner.shape[1]

    def kernel(*refs):
        d_out, d_sec, slope_ref, n_ref, r_ref, wi, wu, wo, vec = refs[:9]
        d_in, d_first, d_attn, sums, d_heads = refs[9:]
        d_first[...] = d_sec[...]
        for cut in range(0, hidden_units, FF_CUT):
            grad = dot_nt(d_out[...], wu[cut : cut + FF_CUT, :])
            grad = (grad * slope_ref[:, cut : cut + FF_CUT]).astype(BF)
            d_in[:, cut : cut + FF_CUT] = grad
            d_first[...] += dot_nt(grad, wi[:, cut : cut + FF_CUT])
        d_hidden = d_first[...]
        n = n_ref[...]
        sums[0:1, :] = jnp.sum(d_hidden * n, axis=0, keepdims=True)
        sums[1:2, :] = jnp.sum(d_hidden, axis=0, keepdims=True)
        first = normal_back(d_hidden * vec[...].reshape(1, width), n, r_ref[:, 0:1])
        d_first[...] = first
        d_attn[...] = first.astype(BF)
        d_heads[...] = dot_nt(d_attn[...], wo[...]).astype(BF)

    return Stage(
        kernel,
        (d_outer, d_second, slope, n_one, r_one, w_inner, w_outer, w_out, gain_one),
        [vmem()] * 9,
        (
            like((rows, hidden_units), BF),
            like((rows, width), F32),
            like((rows, width), BF),
            like((2, width), F32),
            like((rows, width), BF),
        ),
    )


def attn_back(
    d_heads, probs, query, keys_all, values_all, query_at, key_at, first_pair, pairs, spare=0
):
    rows, width = d_heads.shape
    columns = pairs * LANES
    head_count, _, keys = probs.shape
    half_span = REL // 2

    def kernel(*refs):
        d_ref, p_ref, q_ref, k_ref, v_ref, q_at, k_at = refs[:7]
        dkv_ref, tables = refs[7:9]
        heads_t, q_t, line_idx, key_hots, line_hots, row_hots, line_rows, rolls = refs[9:]
        base = first_pair * LANES
        heads_t[...] = d_ref[:, base : base + columns].astype(F32).T.astype(BF)
        q_t[...] = q_ref[:, base : base + columns].astype(F32).T.astype(BF)
        line_idx[...] = line_index(q_at, k_at)
        lane = lax.broadcasted_iota(I32, (rows, LANES), 1)
        sub = lax.broadcasted_iota(I32, (LANES, keys), 0)
        place = jnp.where(sub < BOXES, k_at[2:3, :], k_at[3:4, :])
        key_hots[0:LANES] = ((sub & (BOXES - 1)) == place).astype(F32).astype(BF)
        key_hots[LANES:] = (sub == k_at[0:1, :]).astype(F32).astype(BF)
        line_hots[...] = (sub == (k_at[1:2, :] & (LANES - 1))).astype(F32).astype(BF)
        place = jnp.where(lane < BOXES, q_at[:, 2:3], q_at[:, 3:4])
        row_hots[...] = ((BOXES - 1 - (lane & (BOXES - 1))) == place).astype(F32).T.astype(BF)
        line_rows[...] = (
            ((LANES - 1 - lane) == (q_at[:, 1:2] & (LANES - 1))).astype(F32).T.astype(BF)
        )
        region_hot = (lane == q_at[:, 0:1]).astype(F32)
        tables[...] = jnp.zeros_like(tables)
        rolls[...] = jnp.zeros_like(rolls)
        square_row = lax.broadcasted_iota(I32, (LANES, LANES), 0)
        square_lane = lax.broadcasted_iota(I32, (LANES, LANES), 1)
        one_lane = lax.broadcasted_iota(I32, (1, LANES), 1)
        def rolled(square):
            return jnp.sum(
                pltpu.roll(square, 0, 1, stride=1, stride_axis=0), axis=0, keepdims=True
            )

        def pair(at, carry):
            col = pl.ds(pl.multiple_of(at * LANES, LANES), LANES)
            key_col = pl.ds(pl.multiple_of(base + at * LANES, LANES), LANES)
            d_pair, k_pair, v_pair = d_ref[:, key_col], k_ref[:, key_col], v_ref[:, key_col]
            back = []
            for half in range(2):
                head = 2 * (first_pair + at) + half
                own = pl.ds(pl.multiple_of(at * LANES + 64 * half, 64), 64)
                mine = (lane < 64) if half == 0 else (lane >= 64)
                d_one = jnp.where(mine, d_pair, jnp.zeros_like(d_pair))
                d_probs = dot_nt(d_one, v_pair)
                low_probs = p_ref[head]
                p_one = low_probs.astype(F32)
                row_dot = jnp.sum(p_one * d_probs, axis=1, keepdims=True)
                d_score = p_one * (d_probs - row_dot)
                low_score = d_score.astype(BF)
                back.append(dot_nn(low_score, k_pair))
                below = pl.ds(pl.multiple_of(columns + at * LANES + 64 * half, 64), 64)
                dkv_ref[own, :] = dot_nn(q_t[own, :], low_score).astype(BF)
                dkv_ref[below, :] = dot_nn(heads_t[own, :], low_probs).astype(BF)
                at_keys = dot_nt(low_score, key_hots[...])
                in_region = all_sum(at_keys[:, LANES:] * region_hot)
                boxes = at_keys[:, :LANES]
                whole = all_sum(jnp.where(lane < BOXES, boxes, 0.0))
                high, low = two_parts(boxes)
                square = dot_nn(row_hots[...], high) + dot_nn(row_hots[...], low)
                horiz = rolled(jnp.where((square_row < 64) & (square_lane < 64), square, 0.0))
                vert = pltpu.roll(
                    jnp.where((square_row >= 64) & (square_lane >= 64), square, 0.0),
                    64,
                    1,
                    stride=1,
                    stride_axis=0,
                )
                vert = jnp.sum(vert, axis=0, keepdims=True)
                near = line_idx[...] & (REL - 1)
                wide = low_score.astype(F32)
                inside = jnp.where((near > 0) & (near < REL - 1), wide, 0.0).astype(BF)
                before = all_sum(jnp.where(near == 0, wide, 0.0))
                high, low = two_parts(dot_nt(inside, line_hots[...]))
                square = dot_nn(line_rows[...], high) + dot_nn(line_rows[...], low)
                line = rolled(square)
                within = all_sum(square)
                rolls[0, pl.ds(head, 1), :] = horiz
                rolls[1, pl.ds(head, 1), :] = vert
                rolls[2, pl.ds(head, 1), :] = line
                row = jnp.where(one_lane == 0, before, 0.0)
                row = row + jnp.where(one_lane == REL - 1, whole - before - within, 0.0)
                row = row + jnp.where(one_lane == 3 * REL, in_region, 0.0)
                tables[pl.ds(head, 1), :] = row
            dkv_ref[2 * columns : 2 * columns + rows, col] = (jnp.where(lane < 64, back[0], back[1]) * 0.125).astype(BF)
            return carry

        lax.fori_loop(0, pairs, pair, 0)
        bucket = square_lane & (REL - 1)

        def from_distance(distance):
            return jnp.clip(distance, -half_span, half_span - 1) + half_span

        horiz_map = (
            (from_distance(square_row - (BOXES - 1)) == bucket)
            & (square_lane >= REL)
            & (square_lane < 2 * REL)
        ).astype(F32)
        around = jnp.where(square_row < BOXES, square_row + 1, square_row + 1 - LANES)
        vert_map = (
            (from_distance(around) == bucket)
            & (square_lane >= 2 * REL)
            & (square_lane < 3 * REL)
        ).astype(F32)
        line_map = ((from_distance(around) == bucket) & (square_lane < REL)).astype(F32)

        def exact(left, right):
            return lax.dot_general(
                left,
                right,
                (((1,), (0,)), ((), ())),
                precision=lax.Precision.HIGHEST,
                preferred_element_type=F32,
            )

        tables[...] += (
            exact(rolls[0], horiz_map) + exact(rolls[1], vert_map) + exact(rolls[2], line_map)
        )

    return Stage(
        kernel,
        (d_heads, probs, query, keys_all, values_all, query_at, key_at),
        [vmem()] * 7,
        (
            like((2 * columns + rows + spare, keys), BF),
            like((16, LANES), F32),
        ),
        [
            pltpu.VMEM((columns, rows), BF),
            pltpu.VMEM((columns, rows), BF),
            pltpu.VMEM((rows, keys), I32),
            pltpu.VMEM((2 * LANES, keys), BF),
            pltpu.VMEM((LANES, keys), BF),
            pltpu.VMEM((LANES, rows), BF),
            pltpu.VMEM((LANES, rows), BF),
            pltpu.VMEM((3, 16, LANES), F32),
        ],
    )


def fetch(weights):
    count = len(weights)

    def kernel(*refs):
        copies = [
            pltpu.make_async_copy(far, near, refs[-1].at[at])
            for at, (far, near) in enumerate(zip(refs[:count], refs[count:-1]))
        ]
        for copy in copies:
            copy.start()
        for copy in copies:
            copy.wait()

    return Stage(
        kernel,
        weights,
        [pl.BlockSpec(memory_space=pltpu.HBM)] * count,
        [like(weight.shape, BF) for weight in weights],
        [pltpu.SemaphoreType.DMA((count,))],
    )


def rows_back(d_first, parts, weights, shards):
    rows, width = d_first.shape
    count = width // len(parts)

    def kernel(first, wq, wk, wv, *refs):
        part_refs, (own, send, keep) = refs[: len(parts)], refs[len(parts) :]
        for at in range(shards - 1, -1, -1):
            cut, total = slice(at * rows, (at + 1) * rows), None
            for group, part in enumerate(part_refs):
                col = slice(group * count, (group + 1) * count)
                value = dot_nn(wk[:, col], part[:count, cut])
                value = value + dot_nn(wv[:, col], part[count : 2 * count, cut])
                total = value if total is None else total + value
            if at % 2:
                send[at // 2] = total.T.astype(BF)
            elif at:
                keep[at // 2 - 1] = total.T.astype(BF)
            else:
                result = first[...] + total.T
                for group, part in enumerate(part_refs):
                    d_query = part[2 * count : 2 * count + rows, :count]
                    col = slice(group * count, (group + 1) * count)
                    result = result + dot_nt(d_query, wq[:, col])
                own[...] = result

    return Stage(
        kernel,
        (d_first, *weights, *parts),
        [vmem()] * (4 + len(parts)),
        (
            like((rows, width), F32),
            like((shards // 2, rows, width), BF),
            like((shards // 2 - 1, rows, width), BF),
        ),
    )


def rows_step(own, keep, got):
    def kernel(own_ref, keep_ref, got_ref, out, send):
        out[...] = own_ref[...] + got_ref[0].astype(F32)
        send[...] = keep_ref[0] + got_ref[1]

    return Stage(kernel, (own, keep, got), [vmem()] * 3, (like(own.shape, F32), like(own.shape, BF)))


def rows_result(own, got, row_count):
    def kernel(own_ref, got_ref, out):
        out[...] = (own_ref[...] + got_ref[...].astype(F32))[:row_count].astype(BF)

    return Stage(kernel, (own, got), [vmem()] * 2, (like((row_count, own.shape[1]), BF),))


def two_halves(value):
    high, low = two_parts(value)
    return jnp.concatenate([high.astype(F32), low.astype(F32)], 0)


def pack(sums, tables, spare):
    width = sums[0].shape[1]
    height = sum(item.shape[0] for item in sums) * width // LANES

    def kernel(*refs):
        out, place = refs[-1], 0
        for ref in refs[: len(sums)]:
            for row in range(ref.shape[0]):
                for cut in range(0, width, LANES):
                    out[place : place + 1] = ref[row : row + 1, cut : cut + LANES]
                    place += 1
        total = refs[len(sums)][...]
        for ref in refs[len(sums) + 1 : -2]:
            total = total + ref[...]
        out[place : place + total.shape[0]] = total
        out[place + total.shape[0] :] = jnp.zeros_like(out[place + total.shape[0] :])
        high, low = two_parts(out[...])
        below = refs[-2].shape[0] - high.shape[0]
        refs[-2][below:, :LANES] = high
        refs[-2][below:, LANES : 2 * LANES] = low

    operands = (*sums, *tables, spare)
    return Stage(
        kernel, operands, [vmem()] * len(operands), (like((-(-(height + tables[0].shape[0]) // 16) * 16, LANES), F32),)
    )


def swap(array_in, axis_name, flip):
    size = lax.axis_size(axis_name)
    return lax.ppermute(array_in, axis_name, [(at, at ^ flip) for at in range(size)])


def tok_shards(array_in):
    return [array_in] + [swap(array_in, "tok", step) for step in range(1, lax.axis_size("tok"))]


def whole_value(halves):
    return halves[: halves.shape[0] // 2] + halves[halves.shape[0] // 2 :]


def put_load(out, item, value):
    halves = two_halves(value)
    rows, cols = out.shape[1:]
    count = halves.shape[0] // rows
    for at in range(count):
        low = cols - (count - at) * LANES
        out[item, :, low : low + LANES] = halves[at * rows : (at + 1) * rows].astype(BF)


class Cut:
    def __init__(self, array, low, high):
        self.array, self.low, self.high = array, low, high


def cut_of(right, form):
    if isinstance(right, Cut):
        return right
    return Cut(right, 0, right.shape[form == "nn"])


def xor_terms(groups, cuts, load=None):
    pages = lax.axis_size("page")
    width = groups[0][0].shape[1]
    rows = width // pages
    rights = [cut_of(right, form) for _, right, form in groups]
    cols = [right.high - right.low for right in rights]
    lefts, which = [], []
    for left, _, _ in groups:
        found = [at for at, item in enumerate(lefts) if item is left]
        which.append(found[0] if found else len(lefts))
        if not found:
            lefts.append(left)

    def kernel(*refs):
        if load is not None:
            load_ref, refs = refs[0], refs[1:]
        left_refs = refs[: len(lefts)]
        right_refs = refs[len(lefts) : len(lefts) + len(groups)]
        keep, *sends = refs[len(lefts) + len(groups) :][: 1 + len(cuts)]
        rest = refs[1 + len(cuts) + len(lefts) + len(groups) :]
        turned, picked = rest[: len(lefts)], rest[len(lefts) :]
        for left_ref, turned_ref in zip(left_refs, turned):
            turned_ref[...] = (
                left_ref[...].astype(F32).T.astype(BF).reshape(pages, rows, left_ref.shape[0])
            )
        page = lax.axis_index("page")
        for odd in (1, 0):
            for at, turned_ref in enumerate(turned):
                for step in range(pages // 2):
                    picked[at][step * rows : (step + 1) * rows] = turned_ref[
                        page ^ (2 * step + odd)
                    ]
            place = 0
            outs = [out for out, count in zip(sends, cuts) for _ in range(count)]
            for at_left, right_ref, right, (_, _, form), count, out in zip(
                which, right_refs, rights, groups, cols, outs if odd else [keep] * len(groups)
            ):
                if odd and place and out is not last:
                    place = 0
                last = out
                for cut in range(0, count, 256):
                    end = min(cut + 256, count)
                    used = slice(right.low + cut, right.low + end)
                    if form == "nn":
                        value = dot_nn(picked[at_left][...], right_ref[:, used])
                    else:
                        value = dot_nt(picked[at_left][...], right_ref[used, :])
                    out[:, :, place + cut : place + end] = value.astype(BF).reshape(
                        pages // 2, rows, end - cut
                    )
                place += count
        if load is not None:
            put_load(sends[-1], 0, load_ref[...])

    sizes, first = [sum(cols)], 0
    for count in cuts:
        sizes.append(sum(cols[first : first + count]))
        first += count
    if load is not None:
        sizes[-1] += LANES
    extra = [] if load is None else [load]
    return Stage(
        kernel,
        (
            *extra,
            *lefts,
            *[right.array for right in rights],
        ),
        [vmem()] * (len(extra) + len(lefts) + len(groups)),
        [like((pages // 2, rows, size), BF) for size in sizes],
        [pltpu.VMEM((pages, rows, left.shape[0]), BF) for left in lefts]
        + [pltpu.VMEM((pages // 2 * rows, left.shape[0]), BF) for left in lefts],
    )


def plain_terms(groups):
    pages, parts = lax.axis_size("page"), []
    for left, right, form in groups:
        cut = cut_of(right, form)
        side = int(form == "nn")
        used = lax.slice_in_dim(cut.array, cut.low, cut.high, axis=side)
        part = lax.dot_general(
            left, used, (((0,), (1 - side,)), ((), ())), preferred_element_type=F32
        )
        parts.append(part.astype(BF))
    whole = jnp.concatenate(parts, 1)
    whole = whole.reshape(pages, whole.shape[0] // pages, whole.shape[1])
    whole = jnp.take(whole, lax.axis_index("page") ^ jnp.arange(pages), axis=0)
    return whole[0::2], [whole[1::2]]


def with_terms(stages, sums, name, limit, after=(), load=None, cuts=None):
    width, pages = sums[0][0][0].shape[1], lax.axis_size("page")
    if width // pages % 16:
        outs = run(stages, name, limit, after) if stages else ()
        order = [item for stage in stages for item in stage.results]

        def real(item):
            return outs[order.index(item)] if isinstance(item, Later) else item

        return [
            plain_terms([(real(left), real(right), form) for left, right, form in groups])
            for groups in sums
        ], outs
    last = [xor_terms(groups, cuts or [len(groups)], load) for groups in sums]
    outs = run([*stages, *last], name, limit, after)
    each = 1 + len(cuts or [0])
    count = len(outs) - each * len(sums)
    terms = [(outs[at], list(outs[at + 1 : at + each])) for at in range(count, len(outs), each)]
    return terms, outs[:count]


def plain_sum(pair):
    def kernel(left, right, out):
        out[...] = left[...] + right[...]

    return Stage(kernel, pair, [vmem()] * 2, (like(pair[0].shape, pair[0].dtype),))


class Rider:
    def __init__(self, vector, path):
        self.path = [("page", 1)] + path
        self.move(vector)

    def stage(self):
        return plain_sum(self.pair)

    def move(self, vector):
        self.pair = (vector, swap(vector, *self.path.pop(0)))


def add_columns(kept, got, at, low, high, kind):
    ends = set()
    for pieces in (kept, got):
        place = 0
        for piece in pieces:
            place += piece.shape[-1]
            ends.add(place)
    ends = sorted(end for end in ends if low < end < high) + [high]

    def read(pieces, first, last):
        place = 0
        for piece in pieces:
            if place <= first and last <= place + piece.shape[-1]:
                return piece[(*at, slice(None), slice(first - place, last - place))].astype(kind)
            place += piece.shape[-1]

    values, first = [], low
    for end in ends:
        values.append(read(kept, first, end) + read(got, first, end))
        first = end
    return values[0] if len(values) == 1 else jnp.concatenate(values, 1)


class Reduction:
    def __init__(self, terms, name, turn=False, tok_first=False):
        keep, sends = terms
        pages, toks = lax.axis_size("page"), lax.axis_size("tok")
        self.name, self.count, self.pages, self.toks = name, 0, pages, toks
        bits = [1 << at for at in range(1, pages.bit_length() - 1)]
        page_path = [("page", bit) for bit in (bits[::-1] if turn else bits)]
        tok_path = [("tok", 1 << at) for at in range(toks.bit_length() - 1)]
        self.path = tok_path + page_path if tok_first else page_path + tok_path
        self.labels, self.split = list(range(0, pages, 2)), False
        self.kept, self.got = [keep], [swap(piece, "page", 1) for piece in sends]

    def join(self, other):
        self.kept, self.got = self.kept + other.kept, self.got + other.got

    def step(self, after=(), rider=None, cuts=None):
        begun = self.count > 0
        self.halve(after, rider, cuts)
        while begun and self.path and self.path[0][0] == "page":
            self.halve(after, rider)

    def halve(self, after=(), rider=None, cuts=None):
        axis, bit = self.path.pop(0)
        flag = bit if axis == "page" else bit * self.pages
        first = axis == "tok" and not self.split
        arrays, toks = [*self.kept, *self.got], self.toks
        rows, cols = self.kept[0].shape[1], sum(array.shape[2] for array in self.kept)
        if first:
            rows //= toks
            arrays = [a.reshape(a.shape[0], toks, rows, a.shape[2]) for a in arrays]
            self.labels = [at + self.pages * r for at in self.labels for r in range(toks)]
            self.split = True
        labels = self.labels
        cuts = cuts or [cols]
        send = [at for at, label in enumerate(labels) if label & flag]
        keep = [at for at, label in enumerate(labels) if not label & flag]
        held = len(self.kept)
        kind = BF if self.path else F32

        def kernel(*refs):
            tok = lax.axis_index("tok")
            kept, got = refs[:held], refs[held : len(arrays)]
            keep_out, *outs = refs[len(arrays) :]

            def total(at, low, high, out_kind):
                at = (at // toks, tok ^ (at % toks)) if first else (at,)
                return add_columns(kept, got, at, low, high, out_kind)

            low = 0
            for out, width in zip(outs, cuts):
                for place, at in enumerate(send):
                    out[place] = total(at, low, low + width, BF)
                low += width
            for place, at in enumerate(keep):
                keep_out[place] = total(at, 0, cols, kind)

        stages = [
            Stage(
                kernel,
                arrays,
                [vmem()] * len(arrays),
                [like((len(keep), rows, cols), kind)]
                + [like((len(send), rows, width), BF) for width in cuts],
            )
        ]
        if rider:
            stages.append(rider.stage())
        self.count += 1
        outs = run(stages, f"{self.name}_step{self.count}", 4, after)
        self.labels = [labels[at] for at in keep]
        self.last = outs[0]
        self.kept = [outs[0]]
        self.got = [swap(piece, axis, bit) for piece in outs[1 : 1 + len(cuts)]]
        if rider:
            rider.move(outs[-1])

    def until(self, left, after=(), rider=None):
        while len(self.path) > left:
            self.halve(after, rider)

    def result(self, columns, after=(), side=None):
        held, rows = len(self.kept), self.kept[0].shape[1]
        sides = [] if side is None else [side]
        extra = 0 if side is None else side.shape[1]

        def kernel(*refs):
            ins, outs = refs[: -len(columns)], refs[-len(columns) :]
            kept, got, low = ins[:held], ins[held : held + len(self.got)], 0
            for out, width in zip(outs, columns):
                own = width - (extra if out is outs[-1] else 0)
                out[:, :own] = add_columns(kept, got, (0,), low, low + own, F32)
                low += own
            if sides:
                outs[-1][:, columns[-1] - extra :] = ins[-1][...]

        stage = Stage(
            kernel,
            (*self.kept, *self.got, *sides),
            [vmem()] * (held + len(self.got) + len(sides)),
            [like((rows, width), F32) for width in columns],
        )
        return run([stage], f"{self.name}_result", 4, after)


class Direct:
    def __init__(self, tokens_pair, parts_pair, load, side, rows, name, after):
        pages, toks = lax.axis_size("page"), lax.axis_size("tok")
        items, keys = pages // 2, tokens_pair[0].shape[0]
        share = tokens_pair[0].shape[1] // pages
        cols = 3 * tokens_pair[0].shape[1]
        count = cols // 3 // len(parts_pair)
        extra = side.kept[0].shape[2]
        self.name = name

        def kernel(mine, other, load_ref, side_kept, side_got, *refs):
            part_refs, refs = refs[: 2 * len(parts_pair)], refs[2 * len(parts_pair) :]
            own, load_out, side_own = refs[:3]
            outs, (turned, picked) = refs[3 : 2 + items], refs[2 + items :]
            page = lax.axis_index("page")
            for which, ref in enumerate((mine, other)):
                turned[...] = ref[...].astype(F32).T.astype(BF).reshape(pages, share, keys)
                for at in range(items):
                    picked[which, at * share : (at + 1) * share] = turned[page ^ (2 * at)]
            for group in range(len(parts_pair)):
                for kind in range(3):
                    total = None
                    for which in range(2):
                        part = part_refs[2 * group + which]
                        if kind == 0:
                            d_query = part[2 * count : 2 * count + rows, :count]
                            value = dot_nn(picked[which, :, :rows], d_query)
                        else:
                            used = slice((kind - 1) * count, kind * count)
                            value = dot_nt(picked[which], part[used, :])
                        total = value if total is None else total + value
                    place = kind * (cols // 3) + group * count
                    col = slice(place, place + count)
                    own[:, col] = total[:share]
                    for at in range(1, items):
                        outs[at - 1][0, :, col] = total[at * share : (at + 1) * share].astype(BF)
            below = part_refs[-1]
            height = load_ref.shape[0]
            value = below[-height:, :LANES].astype(F32) + below[-height:, LANES : 2 * LANES].astype(
                F32
            )
            value = whole_value(two_halves(load_ref[...])) + value
            load_out[...] = value
            side_own[...] = side_kept[0].astype(F32) + side_got[0].astype(F32)
            for at in range(1, items):
                outs[at - 1][0, :, cols : cols + extra] = side_kept[at] + side_got[at]
                put_load(outs[at - 1], 0, value)

        flat = [part for pair in parts_pair for part in pair]
        operands = (*tokens_pair, load, side.kept[0], side.got[0], *flat)
        stage = Stage(
            kernel,
            operands,
            [vmem()] * len(operands),
            [
                like((share, cols), F32),
                like(load.shape, F32),
                like((share, extra), F32),
                *[like((1, share, cols + extra + LANES), BF)] * (items - 1),
            ],
            [
                pltpu.VMEM((pages, share, keys), BF),
                pltpu.VMEM((2, items * share, keys), BF),
            ],
        )
        own, self.load, self.side_own, *sends = run([stage], f"{name}_terms", 10, after)
        self.first = own
        self.kept = own.reshape(toks, share // toks, cols)
        self.got = [
            swap(piece, "page", 2 * (at + 1)).reshape(toks, share // toks, cols + extra + LANES)
            for at, piece in enumerate(sends)
        ]

    def along(self, after):
        toks, rows, cols = self.kept.shape
        blocks = 2 * self.load.shape[0] // rows
        extra = self.side_own.shape[1]

        def kernel(kept, load, side_own, one, two, three, own, load_out, side_out, *outs):
            tok = lax.axis_index("tok")
            for at in range(toks):
                total = side_own[at * rows : (at + 1) * rows]
                for piece in (one, two, three):
                    total = total + piece[at, :, cols : cols + extra].astype(F32)
                side_out[at * rows : (at + 1) * rows] = total
            halves = [
                whole_value(piece[:, :, cols + extra :].astype(F32).reshape(toks * rows, LANES))
                for piece in (one, two, three)
            ]
            mine = whole_value(two_halves(load[...]))
            value = (mine + halves[0]) + (halves[1] + halves[2])
            load_out[...] = value
            for step in range(toks):
                at = tok ^ step
                total = kept[at] + one[at, :, :cols].astype(F32)
                total = total + two[at, :, :cols].astype(F32) + three[at, :, :cols].astype(F32)
                if step:
                    outs[step - 1][0, :, :cols] = total.astype(BF)
                    put_load(outs[step - 1], 0, value)
                else:
                    own[...] = total

        stage = Stage(
            kernel,
            (self.kept, self.load, self.side_own, *self.got),
            [vmem()] * 6,
            [
                like((rows, cols), F32),
                like(self.load.shape, F32),
                like((toks * rows, extra), F32),
            ]
            + [like((1, rows, cols + blocks * LANES), BF)] * (toks - 1),
        )
        self.kept, self.load, self.side_sum, *sends = run(
            [stage], f"{self.name}_step2", 6, after
        )
        self.last = self.kept
        self.got = [swap(piece, "tok", at + 1) for at, piece in enumerate(sends)]

    def result(self, columns, after):
        rows, cols = self.kept.shape
        blocks = 2 * self.load.shape[0] // rows

        def kernel(kept, load, one, two, three, load_out, *outs):
            halves = []
            for piece in (one, two, three):
                parts = [
                    piece[0, :, cols + at * LANES :][:, :LANES].astype(F32) for at in range(blocks)
                ]
                halves.append(whole_value(jnp.concatenate(parts, 0)))
            mine = whole_value(two_halves(load[...]))
            load_out[...] = (mine + halves[0]) + (halves[1] + halves[2])
            low = 0
            for out, width in zip(outs, columns):
                cut = slice(low, low + width)
                total = kept[:, cut] + one[0, :, cut].astype(F32)
                out[...] = total + two[0, :, cut].astype(F32) + three[0, :, cut].astype(F32)
                low += width

        stage = Stage(
            kernel,
            (self.kept, self.load, *self.got),
            [vmem()] * 5,
            [like(self.load.shape, F32)] + [like((rows, width), F32) for width in columns],
        )
        load, *outs = run([stage], f"{self.name}_result", 6, after)
        self.last = load
        return outs, load


class Halved:
    def __init__(self, terms, load, name, side):
        self.sum, self.side = Reduction(terms, name), side
        self.first = self.sum.kept[0]
        self.rider = Rider(load, list(self.sum.path))

    def along(self, after):
        self.sum.until(0, after, self.rider)
        self.side.until(0, (self.sum.last,))
        self.last = self.side.last
        self.side_sum = self.side.kept[0][0] + self.side.got[0][0].astype(F32)

    def result(self, columns, after):
        outs = self.sum.result(columns, after)
        self.last = outs[0]
        return outs, self.rider.pair[0] + self.rider.pair[1]


def on_device(
    tokens,
    w_query,
    w_key,
    w_value,
    w_out,
    w_inner,
    w_outer,
    gain_one,
    shift_one,
    gain_two,
    shift_two,
    table_line,
    table_horiz,
    table_vert,
    region_weight,
    region_ids,
    line_pos,
    box_horiz,
    box_vert,
    cotangent,
):
    row_count, width = tokens.shape
    shards = lax.axis_size("tok")
    rows = -(-(row_count + 2) // 16) * 16

    (padded_tokens,) = run(
        [with_places(tokens, (region_ids, line_pos, box_horiz, box_vert), rows)], "places", 4
    )
    token_shards = tok_shards(padded_tokens)
    places = jnp.stack([region_ids, line_pos, box_horiz, box_vert], 1)
    query_at = jnp.pad(places, ((0, rows - row_count), (0, 4)))
    line_table = jnp.concatenate(
        [
            table_line,
            table_line + region_weight[:, None],
            jnp.full((table_line.shape[0], LANES - 2 * REL), NEG, F32),
        ],
        1,
    )
    box_table = jnp.pad(
        jnp.concatenate([table_horiz, table_vert], 1), ((0, 0), (0, LANES - 2 * REL))
    )
    vectors = (gain_one, shift_one, gain_two, shift_two)

    w_query, w_key, w_value, w_out, w_inner, w_outer = run(
        [fetch((w_query, w_key, w_value, w_out, w_inner, w_outer))], "fetch", 1, (padded_tokens,)
    )
    ready = run(
        [first_rows(token_shards[:2], (w_key, w_value, w_query))], "first_rows", 6
    )
    first = attn_forward(
        token_shards,
        row_count,
        ready,
        (w_key, w_value),
        line_table,
        box_table,
        query_at,
    )
    second = feed_forward(
        first.results[0],
        padded_tokens,
        row_count,
        w_out,
        w_inner,
        w_outer,
        vectors,
        cotangent,
    )
    unit = width // 6
    terms, outs = with_terms(
        [first, second],
        [
            [(second.results[4], Cut(second.results[7], 0, 4 * unit), "nn")],
            [(second.results[4], Cut(second.results[7], 4 * unit, width), "nn")],
        ],
        "forward",
        10,
    )
    mix, query, keys_all, values_all, tokens_all, probs, key_at = outs[:7]
    block, hidden, n_one, r_one, active, slope, d_second, d_outer, sums_two = outs[7:]
    outer = Reduction(terms[0], "outer")
    zed = Reduction(terms[1], "zed", tok_first=True)
    back = feed_back(d_outer, d_second, slope, n_one, r_one, w_inner, w_outer, w_out, gain_one)
    d_inner, d_first, d_attn, sums_one, d_heads = run([back], "feed_back", 8, (outer.kept[0],))
    outer.step((d_attn,), cuts=[2 * unit, 2 * unit])
    zed.halve((outer.last,))
    main = 16 * unit
    terms, _ = with_terms(
        [],
        [
            [(hidden, Cut(d_inner, 0, main), "nn")],
            [(hidden, Cut(d_inner, main, w_inner.shape[1]), "nn"), (mix, d_attn, "nn")],
        ],
        "inner_terms",
        10,
        (d_attn, zed.last),
    )
    inner = Reduction(terms[0], "inner", turn=True)
    out = Reduction(terms[1], "out")
    whole_tiles = lax.axis_size("page") == 8 and width // lax.axis_size("page") % 16 == 0
    third = width // LANES // 3

    def heads_back(at, spare=0):
        return attn_back(
            d_heads, probs, query, keys_all, values_all, query_at, key_at, at * third, third, spare
        )

    def beside(array):
        return [swap(array, "page", 1)] if whole_tiles else []

    other_tokens = beside(tokens_all)

    part_one, tables_one = run([heads_back(0)], "attn_back", 10, (out.kept[0], ))
    zed.halve((tables_one, *outer.got[:1]))
    inner.step((zed.last,), cuts=[16 * unit])
    out.step((inner.last,), cuts=[14 * unit])
    others = beside(part_one)
    part_two, tables_two = run(
        [heads_back(1)], "attn_more", 10, (out.last,)
    )
    others += beside(part_two)
    stage = heads_back(2, 48)
    last_part, _, small = run(
        [stage, pack((sums_one, sums_two), (tables_one, tables_two, stage.results[1]), stage.results[0])],
        "attn_rest",
        10,
        (tables_two,),
    )
    parts = [part_one, part_two, last_part]
    others += beside(last_part)

    def attn_sum(after):
        if whole_tiles:
            return Direct(
                (tokens_all, *other_tokens),
                list(zip(parts, others)),
                small,
                zed,
                rows,
                "attn",
                after,
            )
        count = width // len(parts)
        groups = (
            [(padded_tokens, part[2 * count :][:rows, :count], "nn") for part in parts]
            + [(tokens_all, Cut(part, 0, count), "nt") for part in parts]
            + [(tokens_all, Cut(part, count, 2 * count), "nt") for part in parts]
        )
        return Halved(plain_terms(groups), small, "attn", zed)

    outer.step((small,))
    inner.step((outer.last, *others[0:1]))
    d_own, rows_sent, rows_kept = run(
        [rows_back(d_first, parts, (w_query, w_key, w_value), shards)], "rows_back", 10, (inner.last,)
    )
    rows_got = swap(rows_sent, "tok", 1)
    out.step((d_own, *others[1:2]))
    attn = attn_sum((out.last, *outer.got[:3], *inner.got[:2]))
    d_own, rows_sent = run(
        [rows_step(d_own, rows_kept, rows_got)], "rows_step", 4, (attn.first,)
    )
    rows_got = swap(rows_sent, "tok", 2)
    inner.join(out)
    inner.step((d_own,))
    outer.step((inner.last,))
    (d_tokens,) = run([rows_result(d_own, rows_got, row_count)], "rows_result", 4, (outer.last,))
    inner.step((d_tokens,))
    outer.step((inner.last,))
    attn.along((outer.last,))
    grad_inner, grad_out = inner.result([w_inner.shape[1], width], (attn.last,))
    (grad_outer,) = outer.result([width], (grad_inner,), attn.side_sum)
    grad_attn, small = attn.result([width] * 3, (grad_outer,))
    vector_rows = width // LANES
    vector_sums = small[: 4 * vector_rows].reshape(4, width)
    tables = small[4 * vector_rows :][: table_line.shape[0]]
    return (
        block,
        d_tokens,
        *grad_attn,
        grad_out,
        grad_inner,
        grad_outer,
        vector_sums[0],
        vector_sums[1],
        vector_sums[2],
        vector_sums[3],
        tables[:, 0:REL],
        tables[:, REL : 2 * REL],
        tables[:, 2 * REL : 3 * REL],
        tables[:, 3 * REL],
    )


def solution(mesh):
    placed = (
        P(("page", "tok"), None),
        P(),
        P(),
        P(),
        P(),
        P(),
        P(),
        P(),
        P(),
        P(),
        P(),
        P(),
        P(),
        P(),
        P(),
        P(("page", "tok")),
        P(("page", "tok")),
        P(("page", "tok")),
        P(("page", "tok")),
        P(("page", "tok"), None),
    )
    return jax.shard_map(
        on_device,
        mesh=mesh,
        in_specs=placed,
        out_specs=(
            P(("page", "tok"), None),
            P(("page", "tok"), None),
            P(("page", "tok"), None),
            P(("page", "tok"), None),
            P(("page", "tok"), None),
            P(("page", "tok"), None),
            P(("page", "tok"), None),
            P(("page", "tok"), None),
            P(),
            P(),
            P(),
            P(),
            P(),
            P(),
            P(),
            P(),
        ),
        check_vma=False,
    )
```
